32 devices in a mesh: items: 4 (over y, x), seq: 8 (over z, core).
Axes of the slice: x: 2, y: 2, z: 4, core: 2. Of those that a mesh axis runs over, the one named last changes fastest.
Arguments:
- features: float32 [4, 4096, 1024], P('items', 'seq'), may hold values from -6 to 6
- item_spans: int32 [4, 8], P('items'), may hold values from 0 to 3, as said below
- item_lengths: int32 [4, 8], P('items'), may hold values from 0 to 1500, as said below
- ffn1_gain: bfloat16 [1024], P(('items', 'seq')), may hold values from 0.25 to 1.75
- ffn1_in: bfloat16 [1024, 4096], P(('items', 'seq')), may hold values from -0.1875 to 0.1875
- ffn1_out: bfloat16 [4096, 1024], P(('items', 'seq')), may hold values from -0.09375 to 0.09375
- att_gain: bfloat16 [1024], P(('items', 'seq')), may hold values from 0.25 to 1.75
- w_query: bfloat16 [1024, 1024], P(('items', 'seq')), may hold values from -0.1875 to 0.1875
- w_key: bfloat16 [1024, 1024], P(('items', 'seq')), may hold values from -0.1875 to 0.1875
- w_value: bfloat16 [1024, 1024], P(('items', 'seq')), may hold values from -0.1875 to 0.1875
- w_pos: bfloat16 [1024, 1024], P(('items', 'seq')), may hold values from -0.1875 to 0.1875
- u_bias: bfloat16 [1024], P(('items', 'seq')), may hold values from -3 to 3
- v_bias: bfloat16 [1024], P(('items', 'seq')), may hold values from -3 to 3
- w_out: bfloat16 [1024, 1024], P(('items', 'seq')), may hold values from -1.5 to 1.5
- conv_gain: bfloat16 [1024], P(('items', 'seq')), may hold values from 0.25 to 1.75
- conv_in: bfloat16 [1024, 2048], P(('items', 'seq')), may hold values from -0.1875 to 0.1875
- depth_kernel: bfloat16 [31, 1024], P(None, ('items', 'seq')), may hold values from -1 to 1
- inner_gain: bfloat16 [1024], P(('items', 'seq')), may hold values from 0.25 to 1.75
- conv_out: bfloat16 [1024, 1024], P(('items', 'seq')), may hold values from -0.1875 to 0.1875
- ffn2_gain: bfloat16 [1024], P(('items', 'seq')), may hold values from 0.25 to 1.75
- ffn2_in: bfloat16 [1024, 4096], P(('items', 'seq')), may hold values from -0.1875 to 0.1875
- ffn2_out: bfloat16 [4096, 1024], P(('items', 'seq')), may hold values from -0.09375 to 0.09375
- final_gain: bfloat16 [1024], P(('items', 'seq')), may hold values from 0.25 to 1.75
- cotangent: float32 [4, 4096, 1024], P('items', 'seq'), may hold values from -6 to 6
Outputs:
- layer_out: float32 [4, 4096, 1024], P('items', 'seq')
- input_grad: float32 [4, 4096, 1024], P('items', 'seq')
- grad_ffn1_gain: float32 [1024], P(('items', 'seq'))
- grad_ffn1_in: float32 [1024, 4096], P(('items', 'seq'))
- grad_ffn1_out: float32 [4096, 1024], P(('items', 'seq'))
- grad_att_gain: float32 [1024], P(('items', 'seq'))
- grad_w_query: float32 [1024, 1024], P(('items', 'seq'))
- grad_w_key: float32 [1024, 1024], P(('items', 'seq'))
- grad_w_value: float32 [1024, 1024], P(('items', 'seq'))
- grad_w_pos: float32 [1024, 1024], P(('items', 'seq'))
- grad_u_bias: float32 [1024], P(('items', 'seq'))
- grad_v_bias: float32 [1024], P(('items', 'seq'))
- grad_w_out: float32 [1024, 1024], P(('items', 'seq'))
- grad_conv_gain: float32 [1024], P(('items', 'seq'))
- grad_conv_in: float32 [1024, 2048], P(('items', 'seq'))
- grad_depth_kernel: float32 [31, 1024], P(None, ('items', 'seq'))
- grad_inner_gain: float32 [1024], P(('items', 'seq'))
- grad_conv_out: float32 [1024, 1024], P(('items', 'seq'))
- grad_ffn2_gain: float32 [1024], P(('items', 'seq'))
- grad_ffn2_in: float32 [1024, 4096], P(('items', 'seq'))
- grad_ffn2_out: float32 [4096, 1024], P(('items', 'seq'))
- grad_final_gain: float32 [1024], P(('items', 'seq'))
The draws below stay inside these ranges and needn't reach their ends.
Inputs may be any that keep to these rules, and one draw needn't show every extreme that they name: `item_spans`: in each group every block either starts an item, holding its number of blocks (3 or 2 for a long item, 1 for a short one in this block alone), or holds 0 and continues the item started before it. Block 0 starts a long item, a long item of 3 blocks starts at block 3 or 2, and the last block ends a long item. `item_lengths`: valid frames of the item that starts in a block: 1025 to 1500 for an item of 3 blocks, 768 to 1024 for one of 2 blocks, 125 to 500 for a short one, 0 in blocks that continue an item. The item of 3 blocks near the middle has exactly 1500.
All inputs are finite; a program needn't handle non-finite values.
Results may differ from the reference program's by a relative error of at most 0.018.
Values may be sent and summed in bfloat16 or wider, within the bound.
A program may use at most 384 MiB of HBM per device.

```python
import jax
import jax.numpy as jnp
from jax import lax

D = 1024
HEAD_DIM = 64
FF = 4096
TAPS = 31
BLOCK = 512
LONG_LEN = 1500
SHORT_LEN = 500
GROUPS = 4
FRAMES = 4096
BLOCKS = 8


def layout(base_key):

    def one_group(group_key):
        coin_key, pick_key, long_key, pair_key, short_key = jax.random.split(group_key, 5)
        coins_all = jax.random.randint(coin_key, (BLOCKS,), 0, 2)
        picks = jax.random.randint(pick_key, (3,), 0, 2)
        middle_start = (BLOCKS // 2 - 1 - picks[0]).astype(jnp.int32)
        first_span = jnp.minimum(2 + picks[1], middle_start).astype(jnp.int32)
        last_span = jnp.minimum(2 + picks[2], BLOCKS - middle_start - 3).astype(jnp.int32)
        last_start = (BLOCKS - last_span).astype(jnp.int32)

        def advance(remain, position):
            begins = remain == 0
            bound_next = jnp.where(position < middle_start, middle_start, last_start)
            roomy = position + 3 <= bound_next
            free_span = jnp.where((coins_all[position] == 1) & roomy, 3, 1)
            chosen = jnp.where(position == 0, first_span, jnp.where(position == middle_start, 3, jnp.where(position == last_start, last_span, free_span)))
            span_now = jnp.where(begins, chosen, 0).astype(jnp.int32)
            remain_next = jnp.where(begins, span_now - 1, remain - 1).astype(jnp.int32)
            return (remain_next, span_now)
        unused_rest, span_row = lax.scan(advance, jnp.int32(0), jnp.arange(BLOCKS, dtype=jnp.int32))
        places = jnp.arange(BLOCKS, dtype=jnp.int32)
        long_len = jax.random.randint(long_key, (BLOCKS,), 2 * BLOCK + 1, LONG_LEN + 1)
        pair_len = jax.random.randint(pair_key, (BLOCKS,), 3 * BLOCK // 2, 2 * BLOCK + 1)
        short_len = jax.random.randint(short_key, (BLOCKS,), SHORT_LEN // 4, SHORT_LEN + 1)
        long_len = jnp.where(places == middle_start, LONG_LEN, long_len)
        length_row = jnp.where(span_row == 3, long_len, jnp.where(span_row == 2, pair_len, jnp.where(span_row == 1, short_len, 0)))
        return (span_row.astype(jnp.int32), length_row.astype(jnp.int32))
    group_keys = jax.random.split(base_key, GROUPS)
    return jax.vmap(one_group)(group_keys)


def draw_item_spans(key, part):
    span_all, length_all = layout(key)
    return span_all


def draw_item_lengths(key, part):
    span_all, length_all = layout(key)
    return length_all


def shard_levels(rng, shape, shards, low, largest):
    gain = 1.0
    for axis_at, parts in shards:
        steps = jax.random.uniform(jax.random.fold_in(jax.random.fold_in(rng, 6), axis_at), (parts,), jnp.float32, low / len(shards), largest / len(shards))
        gain = gain * jnp.repeat(jnp.exp(steps), shape[axis_at] // parts).reshape((-1,) + (1,) * (len(shape) - 1 - axis_at))
    return gain


def scatter_about(rng, shape, scale, reach, shards=(), held_as=jnp.bfloat16):
    entries = jax.random.normal(rng, shape, jnp.float32) * scale
    if len(shards) > 0:
        entries = shard_levels(rng, shape, shards, -0.22, 0.18) * entries
    return jnp.clip(entries, min=-reach, max=reach).astype(held_as)


def setup_inputs(seed: int = 0) -> dict:
    arg_keys = jax.random.split(jax.random.key(seed), 25)
    return {
        "features": scatter_about(arg_keys[0], (GROUPS, FRAMES, D), 1.0, 6.0, ((0, 4), (1, 8)), jnp.float32),
        "item_spans": draw_item_spans(jax.random.fold_in(arg_keys[24], 71), 0),
        "item_lengths": draw_item_lengths(jax.random.fold_in(arg_keys[24], 71), 0),
        "ffn1_gain": jnp.clip(1.0 + 0.15 * jax.random.normal(arg_keys[3], (D,), jnp.float32), 0.25, 1.75).astype(jnp.bfloat16),
        "ffn1_in": scatter_about(arg_keys[4], (D, FF), D ** -0.5, 0.1875, ((0, 32),)),
        "ffn1_out": scatter_about(arg_keys[5], (FF, D), FF ** -0.5, 0.09375, ((0, 32),)),
        "att_gain": jnp.clip(1.0 + 0.15 * jax.random.normal(arg_keys[6], (D,), jnp.float32), 0.25, 1.75).astype(jnp.bfloat16),
        "w_query": scatter_about(arg_keys[7], (D, D), D ** -0.5, 0.1875, ((0, 32),)),
        "w_key": scatter_about(arg_keys[8], (D, D), D ** -0.5, 0.1875, ((0, 32),)),
        "w_value": scatter_about(arg_keys[9], (D, D), D ** -0.5, 0.1875, ((0, 32),)),
        "w_pos": scatter_about(arg_keys[10], (D, D), D ** -0.5, 0.1875, ((0, 32),)),
        "u_bias": scatter_about(arg_keys[11], (D,), 0.5, 3.0, ((0, 32),)),
        "v_bias": scatter_about(arg_keys[12], (D,), 0.5, 3.0, ((0, 32),)),
        "w_out": scatter_about(arg_keys[13], (D, D), (D // 64) ** -0.5, 1.5, ((0, 32),)),
        "conv_gain": jnp.clip(1.0 + 0.15 * jax.random.normal(arg_keys[14], (D,), jnp.float32), 0.25, 1.75).astype(jnp.bfloat16),
        "conv_in": scatter_about(arg_keys[15], (D, 2 * D), D ** -0.5, 0.1875, ((0, 32),)),
        "depth_kernel": scatter_about(arg_keys[16], (TAPS, D), TAPS ** -0.5, 1.0, ((1, 32),)),
        "inner_gain": jnp.clip(1.0 + 0.15 * jax.random.normal(arg_keys[17], (D,), jnp.float32), 0.25, 1.75).astype(jnp.bfloat16),
        "conv_out": scatter_about(arg_keys[18], (D, D), D ** -0.5, 0.1875, ((0, 32),)),
        "ffn2_gain": jnp.clip(1.0 + 0.15 * jax.random.normal(arg_keys[19], (D,), jnp.float32), 0.25, 1.75).astype(jnp.bfloat16),
        "ffn2_in": scatter_about(arg_keys[20], (D, FF), D ** -0.5, 0.1875, ((0, 32),)),
        "ffn2_out": scatter_about(arg_keys[21], (FF, D), FF ** -0.5, 0.09375, ((0, 32),)),
        "final_gain": jnp.clip(1.0 + 0.15 * jax.random.normal(arg_keys[22], (D,), jnp.float32), 0.25, 1.75).astype(jnp.bfloat16),
        "cotangent": scatter_about(arg_keys[23], (GROUPS, FRAMES, D), 1.0, 6.0, ((0, 4), (1, 8)), jnp.float32),
    }


@jax.custom_vjp
def low(v):
    return lax.optimization_barrier(v.astype(jnp.bfloat16)).astype(jnp.float32)

@jax.custom_vjp
def low_back(v):
    return v

def low_keep(v):
    return (low(v), None)

def low_pass(kept, grad):
    return (grad,)

def back_keep(v):
    return (v, None)

def back_low(kept, grad):
    return (low(grad),)
low.defvjp(low_keep, low_pass)
low_back.defvjp(back_keep, back_low)
EPSILON = 1e-05

def product(left_side, right_side):
    return jnp.dot(left_side, right_side, precision=lax.Precision.HIGHEST, preferred_element_type=jnp.float32)

def layer_norm(values, norm_gain):
    center = values - lax.optimization_barrier(jnp.mean(values, axis=-1, keepdims=True))
    spread = lax.optimization_barrier(jnp.mean(center * center, axis=-1, keepdims=True))
    return center * lax.rsqrt(spread + EPSILON) * norm_gain

def block_layout(span_row, length_row):
    places = jnp.arange(span_row.shape[0], dtype=jnp.int32)
    item_start = lax.cummax(jnp.where(span_row > 0, places, 0).astype(jnp.int32), axis=0)
    item_length = jnp.take(length_row, item_start)
    return (item_start, item_length)

def frame_items(frame_index, item_start, item_length, extent):
    inside = (frame_index >= 0) & (frame_index < extent)
    block_index = jnp.clip(frame_index // BLOCK, 0, item_start.shape[0] - 1).astype(jnp.int32)
    owner_item = jnp.take(item_start, block_index)
    valid_frame = inside & (frame_index - owner_item * BLOCK < jnp.take(item_length, block_index))
    return (jnp.where(inside, owner_item, -1).astype(jnp.int32), valid_frame)

def same_item(owners_wide, extent):
    half_taps = (TAPS - 1) // 2
    center = owners_wide[half_taps:half_taps + extent]
    columns = [owners_wide[tap_index:tap_index + extent] == center for tap_index in range(TAPS)]
    return jnp.stack(columns, axis=1).astype(jnp.float32)

def relative_table(model_width):
    distance = (3 * BLOCK - 1 - jnp.arange(6 * BLOCK)).astype(jnp.float32)
    frequency = 1.0 / 10000.0 ** (jnp.arange(0, model_width, 2).astype(jnp.float32) / model_width)
    angles = distance[:, None] * frequency[None, :]
    return jnp.concatenate([jnp.sin(angles), jnp.cos(angles)], axis=1)

def relative_shift(positional):
    flattened = positional.reshape(-1)
    diagonal_band = lax.slice(flattened, (BLOCK - 1,), (BLOCK - 1 + BLOCK * (2 * BLOCK - 1),))
    return diagonal_band.reshape(BLOCK, 2 * BLOCK - 1)[:, :BLOCK]

def attend_head(queries, keys_h, values_h, content_bias, position_bias, relative, item_start, item_length):
    frames = queries.shape[0]
    block_count = frames // BLOCK
    factor = HEAD_DIM ** (-0.5)
    key_bias = lax.optimization_barrier(jnp.sum(keys_h * content_bias, axis=1))
    rel_bias = lax.optimization_barrier(jnp.sum(relative * position_bias, axis=1))
    offsets = jnp.arange(BLOCK, dtype=jnp.int32)

    def one_block(block_index):
        query_rows = lax.dynamic_slice_in_dim(queries, block_index * BLOCK, BLOCK, 0)
        first_block = jnp.take(item_start, block_index)
        item_frames = jnp.take(item_length, block_index)
        score_parts = []
        value_parts = []
        for step_index in range(3):
            key_block = jnp.minimum(first_block + step_index, block_count - 1)
            key_rows = lax.dynamic_slice_in_dim(keys_h, key_block * BLOCK, BLOCK, 0)
            value_rows = lax.dynamic_slice_in_dim(values_h, key_block * BLOCK, BLOCK, 0)
            bias_rows = lax.dynamic_slice_in_dim(key_bias, key_block * BLOCK, BLOCK, 0)
            content = product(query_rows, key_rows.T) + bias_rows[None, :]
            distance_base = jnp.clip((block_index - key_block) * BLOCK, -2 * BLOCK, 2 * BLOCK)
            window = lax.dynamic_slice_in_dim(relative, 2 * BLOCK - distance_base, 2 * BLOCK, 0)
            window_bias = lax.dynamic_slice_in_dim(rel_bias, 2 * BLOCK - distance_base, 2 * BLOCK, 0)
            positional = product(query_rows, window.T) + window_bias[None, :]
            raw_score = low_back(content + relative_shift(positional)) * factor
            key_live = step_index * BLOCK + offsets < item_frames
            score_parts.append(jnp.where(key_live[None, :], raw_score, -1000000000.0))
            value_parts.append(value_rows)
        scores = jnp.concatenate(score_parts, axis=1)
        highest = lax.optimization_barrier(jnp.max(scores, axis=1, keepdims=True))
        weights = jnp.exp(scores - highest)
        shares = weights / lax.optimization_barrier(jnp.sum(weights, axis=1, keepdims=True))
        return product(low(shares), jnp.concatenate(value_parts, axis=0))
    blocks_out = lax.map(jax.checkpoint(one_block), jnp.arange(block_count, dtype=jnp.int32))
    return blocks_out.reshape(frames, queries.shape[1])

def all_heads(queries, keys_all, values_all, content_bias, position_bias, relative, item_start, item_length):
    heads_here = queries.shape[1] // HEAD_DIM

    def split_heads(matrix):
        return matrix.reshape(matrix.shape[0], heads_here, HEAD_DIM).transpose(1, 0, 2)

    def per_head(pieces):
        return attend_head(pieces[0], pieces[1], pieces[2], pieces[3], pieces[4], pieces[5], item_start, item_length)
    result = lax.map(per_head, (split_heads(queries), split_heads(keys_all), split_heads(values_all), content_bias.reshape(heads_here, HEAD_DIM), position_bias.reshape(heads_here, HEAD_DIM), split_heads(relative)))
    return result.transpose(1, 0, 2).reshape(queries.shape[0], heads_here * HEAD_DIM)

def feed_forward(values, norm_gain, in_weight, out_weight):
    hidden = low(layer_norm(values, norm_gain))
    gate_pre = low_back(product(hidden, in_weight))
    active = low(jax.nn.silu(gate_pre))
    return 0.5 * low_back(product(active, out_weight))

def attention_inputs(values, norm_gain, query_weight, key_weight, value_weight):
    hidden = low(layer_norm(values, norm_gain))
    return (low_back(low(product(hidden, query_weight))), low_back(low(product(hidden, key_weight))), low_back(low(product(hidden, value_weight))))

def attention_output(mixed_in, out_weight):
    return low_back(product(mixed_in, out_weight))

def conv_inputs(values, norm_gain, wide_weight, live_mask):
    hidden = low(layer_norm(values, norm_gain))
    doubled = low_back(product(hidden, wide_weight))
    half_width = doubled.shape[1] // 2
    gated = doubled[:, :half_width] * jax.nn.sigmoid(doubled[:, half_width:])
    return low(gated * live_mask[:, None])

def depthwise(extended, kernel, same_mask):
    half_taps = (TAPS - 1) // 2
    extent = extended.shape[0] - 2 * half_taps
    result = jnp.zeros((extent, extended.shape[1]), jnp.float32)
    for tap_index in range(TAPS):
        result = result + kernel[tap_index] * extended[tap_index:tap_index + extent] * same_mask[half_taps:half_taps + extent, tap_index:tap_index + 1]
    return result

def conv_outputs(depth_in, norm_gain, out_weight):
    active = low(jax.nn.silu(layer_norm(depth_in, norm_gain)))
    return low_back(product(active, out_weight))

def conformer(features, item_start, item_length, table_low, params):
    ffn1_gain, ffn1_in, ffn1_out, att_gain, w_query, w_key, w_value, w_pos, u_bias, v_bias, w_out, conv_gain, conv_in, depth_kernel, inner_gain, conv_out, ffn2_gain, ffn2_in, ffn2_out, final_gain = params
    frames = features.shape[0]
    half_taps = (TAPS - 1) // 2
    owners_wide, unused_valid = frame_items((jnp.arange(frames + 4 * half_taps) - 2 * half_taps).astype(jnp.int32), item_start, item_length, frames)
    same_mask = same_item(owners_wide, frames + 2 * half_taps)
    unused_owner, valid_frame = frame_items(jnp.arange(frames, dtype=jnp.int32), item_start, item_length, frames)
    live_mask = valid_frame.astype(jnp.float32)
    first = features + feed_forward(features, ffn1_gain, ffn1_in, ffn1_out)
    queries, keys_all, values_all = attention_inputs(first, att_gain, w_query, w_key, w_value)
    relative = low_back(low(product(table_low, w_pos)))
    mixed = low_back(low(all_heads(queries, keys_all, values_all, u_bias, v_bias, relative, item_start, item_length)))
    second = first + attention_output(mixed, w_out)
    glu_out = conv_inputs(second, conv_gain, conv_in, live_mask)
    padded = jnp.pad(glu_out, ((half_taps, half_taps), (0, 0)))
    depth_out = low_back(depthwise(padded, depth_kernel, same_mask))
    third = second + conv_outputs(depth_out, inner_gain, conv_out)
    fourth = third + feed_forward(third, ffn2_gain, ffn2_in, ffn2_out)
    return layer_norm(fourth, final_gain)

def reference(features, item_spans, item_lengths, ffn1_gain, ffn1_in, ffn1_out, att_gain, w_query, w_key, w_value, w_pos, u_bias, v_bias, w_out, conv_gain, conv_in, depth_kernel, inner_gain, conv_out, ffn2_gain, ffn2_in, ffn2_out, final_gain, cotangent):
    params = tuple((weight.astype(jnp.float32) for weight in (ffn1_gain, ffn1_in, ffn1_out, att_gain, w_query, w_key, w_value, w_pos, u_bias, v_bias, w_out, conv_gain, conv_in, depth_kernel, inner_gain, conv_out, ffn2_gain, ffn2_in, ffn2_out, final_gain)))
    table_low = low(relative_table(D))

    def forward(inputs, weights_all):

        def one_group(pieces):
            item_start, item_length = block_layout(pieces[1], pieces[2])
            return conformer(pieces[0], item_start, item_length, table_low, weights_all)
        return lax.map(one_group, (inputs, item_spans, item_lengths))
    layer_out, pull_back = jax.vjp(forward, features, params)
    input_grad, weight_grads = pull_back(cotangent)
    g_ffn1_gain, g_ffn1_in, g_ffn1_out, g_att_gain, g_w_query, g_w_key, g_w_value, g_w_pos, g_u_bias, g_v_bias, g_w_out, g_conv_gain, g_conv_in, g_depth_kernel, g_inner_gain, g_conv_out, g_ffn2_gain, g_ffn2_in, g_ffn2_out, g_final_gain = weight_grads
    return (layer_out, input_grad, g_ffn1_gain, g_ffn1_in, g_ffn1_out, g_att_gain, g_w_query, g_w_key, g_w_value, g_w_pos, g_u_bias, g_v_bias, g_w_out, g_conv_gain, g_conv_in, g_depth_kernel, g_inner_gain, g_conv_out, g_ffn2_gain, g_ffn2_in, g_ffn2_out, g_final_gain)
```

```python
import functools
import math

import jax
import jax.numpy as jnp
from jax import lax
from jax.experimental import pallas as pl
from jax.experimental.pallas import tpu as pltpu
from jax.sharding import PartitionSpec as P

HEAD_DIM = 64
TAPS = 31
BLOCK = 512
HALF = (TAPS - 1) // 2
EPSILON = 1e-05
NEAR = 3
KEYS = NEAR * BLOCK
RELS = 4 * BLOCK
LANES = 128
ROWS = 128
WINDOW = KEYS + LANES
BF = jnp.bfloat16
F32 = jnp.float32
AXES = ("items", "seq")
SMALL = 128


def dot(left, right):
    return jnp.dot(left, right, preferred_element_type=F32)


def dot_nt(left, right):
    return lax.dot_general(left, right, (((1,), (1,)), ((), ())), preferred_element_type=F32)


def dot_tn(left, right):
    return lax.dot_general(left, right, (((0,), (0,)), ((), ())), preferred_element_type=F32)


def tile_cut(group):
    near = LANES - 4 - 8 * group
    upper = lax.broadcasted_iota(jnp.int32, (8, LANES), 0) < 4
    lane = lax.broadcasted_iota(jnp.int32, (8, LANES), 1)
    return near, near - 4, upper, lane


def own_lanes(half):
    return lax.broadcasted_iota(jnp.int32, (1, LANES), 1) // HEAD_DIM == half


def twice(values, own):
    return jnp.where(own, values, pltpu.roll(values, HEAD_DIM, 1))


def slotted(values):
    row = lax.broadcasted_iota(jnp.int32, values.shape, 0)
    slot = lax.broadcasted_iota(jnp.int32, values.shape, 1) // HEAD_DIM
    place = 3 - row % 4
    return jnp.concatenate(
        [jnp.where(slot == place, values, 0.0), jnp.where(slot + 2 == place, values, 0.0)], axis=1
    ).astype(BF)


def four_rows(r_ref, r_scr, own):
    r_scr[0:RELS, :] = twice(r_ref[...].astype(F32), own)
    r_scr[RELS : RELS + 8, :] = jnp.zeros((8, LANES), F32)
    low = lax.broadcasted_iota(jnp.int32, (1, LANES), 1) < HEAD_DIM
    return jnp.concatenate(
        [
            jnp.where(low, r_scr[s : s + RELS, :], r_scr[s + 1 : s + 1 + RELS, :]).astype(BF)
            for s in (0, 2)
        ],
        axis=1,
    )


def positions_kernel(q_ref, r_ref, b_ref, out_ref, pos_scr, r_scr):
    own = own_lanes(pl.program_id(1))
    qb = (q_ref[...].astype(F32) + b_ref[...].astype(F32)) * HEAD_DIM**-0.5
    pos_scr[...] = dot_nt(slotted(twice(qb, own)), four_rows(r_ref, r_scr, own))

    def chunk(c, carry):
        first = (BLOCK // ROWS - 1 - c) * LANES
        for group in range(ROWS // 8):
            rows = pl.ds(pl.multiple_of(c * ROWS + 8 * group, 8), 8)
            near, far, upper, lane = tile_cut(group)
            stay = lane < LANES - jnp.where(upper, near, far)
            before = None
            for j in range(WINDOW // LANES):
                tile = pos_scr[rows, pl.ds(pl.multiple_of(first + j * LANES, LANES), LANES)]
                moved = jnp.where(
                    upper,
                    pltpu.roll(tile, LANES - near, 1),
                    pltpu.roll(tile, LANES - far, 1) if far else tile,
                )
                if j:
                    out_ref[0, rows, (j - 1) * LANES : j * LANES] = jnp.where(stay, before, moved)
                before = moved
        return carry

    lax.fori_loop(0, BLOCK // ROWS, chunk, 0)


def attend_kernel(
    live_ref, q_ref, k_ref, v_ref, u_ref, pos_ref, mix_ref, e_ref, inv_ref, s_scr, sum_scr, top_scr
):
    half = pl.program_id(1)
    own = own_lanes(half)
    scale = HEAD_DIM**-0.5
    q = q_ref[...].astype(F32)
    qm = jnp.where(own, q * scale, 0.0).astype(BF)
    um = jnp.broadcast_to(jnp.where(own, u_ref[...].astype(F32) * scale, 0.0), q.shape).astype(BF)
    k = k_ref[...]
    s_scr[...] = dot_nt(jnp.concatenate([qm, um], axis=1), jnp.concatenate([k, k], axis=1))
    keep = lax.broadcasted_iota(jnp.int32, (1, KEYS), 1) < live_ref[0]
    mask = jnp.where(keep, 0.0, -1000000000.0)

    def chunk(c, carry):
        for group in range(ROWS // 8):
            rows = pl.ds(pl.multiple_of(c * ROWS + 8 * group, 8), 8)
            top = None
            for j in range(KEYS // LANES):
                at = slice(j * LANES, (j + 1) * LANES)
                score = s_scr[rows, at] + mask[:, at] + pos_ref[0, rows, at]
                sum_scr[rows, at] = score
                top = score if top is None else jnp.maximum(top, score)
            top_scr[8 * group : 8 * group + 8, :] = top
        tops = jnp.max(top_scr[...], axis=1, keepdims=True)
        for pair in range(ROWS // 16):
            rows = pl.ds(pl.multiple_of(c * ROWS + 16 * pair, 16), 16)
            e_ref[0, rows, :] = jnp.exp(sum_scr[rows, :] - tops[16 * pair : 16 * pair + 16]).astype(BF)
        return carry

    lax.fori_loop(0, BLOCK // ROWS, chunk, 0)
    ones = jnp.where(own, v_ref[...].astype(F32), 1.0).astype(BF)
    both = dot(e_ref[0], ones)
    inverse = 1.0 / pltpu.roll(both, HEAD_DIM, 1)
    mixed = both * inverse

    @pl.when(half == 0)
    def _():
        mix_ref[...] = mixed.astype(BF)
        inv_ref[...] = inverse

    @pl.when(half == 1)
    def _():
        mix_ref[...] = jnp.where(own, mixed, mix_ref[...].astype(F32)).astype(BF)
        inv_ref[...] = jnp.where(own, inverse, inv_ref[...])


def pair_block(rows):
    return pl.BlockSpec((rows, LANES), lambda i, h: (0, i))


def head_block(frames):
    return pl.BlockSpec((1, frames, KEYS), lambda i, h: (2 * i + h, 0, 0))


def heads_call(kernel, name, ins, outs, scratch, flops, exps=0):
    pairs = next(a.shape[1] for a, _ in ins if a.ndim == 2) // LANES
    moved = sum(math.prod(a.shape) * a.dtype.itemsize for a, _ in ins)
    moved += sum(math.prod(shape) * jnp.dtype(dtype).itemsize for shape, dtype, _ in outs)
    return pl.pallas_call(
        kernel,
        grid=(pairs, 2),
        in_specs=[spec for _, spec in ins],
        out_specs=[spec for _, _, spec in outs],
        out_shape=[jax.ShapeDtypeStruct(shape, dtype) for shape, dtype, _ in outs],
        scratch_shapes=[pltpu.VMEM(shape, dtype) for shape, dtype in scratch],
        compiler_params=pltpu.CompilerParams(vmem_limit_bytes=48 * 1024 * 1024),
        cost_estimate=pl.CostEstimate(
            flops=8 * flops * 2 * pairs, bytes_accessed=moved, transcendentals=exps * 2 * pairs
        ),
        name=name,
    )(*[a for a, _ in ins])


def relative_scores(q, rel, b):
    frames, width = q.shape
    return heads_call(
        positions_kernel,
        "positions",
        [(q, pair_block(frames)), (rel, pair_block(RELS)), (b, pair_block(1))],
        [((width // HEAD_DIM, frames, KEYS), F32, head_block(frames))],
        [((frames, RELS), F32), ((RELS + 8, LANES), F32)],
        frames * RELS * LANES,
    )[0]


def attend(live, q, k, v, u, relative):
    frames, width = q.shape
    return heads_call(
        attend_kernel,
        "attend",
        [
            (live, pl.BlockSpec(memory_space=pltpu.SMEM)),
            (q, pair_block(frames)),
            (k, pair_block(KEYS)),
            (v, pair_block(KEYS)),
            (u, pair_block(1)),
            (relative, head_block(frames)),
        ],
        [
            ((frames, width), BF, pair_block(frames)),
            ((width // HEAD_DIM, frames, KEYS), BF, head_block(frames)),
            ((frames, width), F32, pair_block(frames)),
        ],
        [((frames, KEYS), F32), ((frames, KEYS), F32), ((ROWS, LANES), F32)],
        2 * frames * KEYS * LANES,
        frames * KEYS,
    )


def keys_back_kernel(
    q_ref, v_ref, u_ref, g_ref, mix_ref, inv_ref, e_ref, ds_ref, dk_ref, dv_ref, dp_scr
):
    frames = q_ref.shape[0]
    qu = (q_ref[...].astype(F32) + u_ref[...].astype(F32)) * HEAD_DIM**-0.5
    grad = g_ref[...].astype(F32) * inv_ref[...]
    lane = lax.broadcasted_iota(jnp.int32, (1, LANES), 1)
    minus = jnp.broadcast_to(jnp.where(lane < 2, -1.0, 0.0), (KEYS, LANES)).astype(BF)
    wide_v = jnp.concatenate([v_ref[...], minus], axis=1)
    qus, gms = [], []
    for half in range(2):
        own = own_lanes(half)
        qus.append(jnp.where(own, qu, 0.0).astype(BF))
        gm = jnp.where(own, grad, 0.0).astype(BF)
        total = jnp.sum(gm.astype(F32) * mix_ref[...].astype(F32), axis=1, keepdims=True)
        high = total.astype(BF).astype(F32)
        totals = jnp.where(lane == 0, high, jnp.where(lane == 1, total - high, 0.0)).astype(BF)
        dp_scr[half] = dot_nt(jnp.concatenate([gm, totals], axis=1), wide_v)
        gms.append(gm)
    gm = jnp.concatenate(gms, axis=0)
    both = e_ref[...].reshape(2 * frames, KEYS)
    dv_ref[...] = dot_tn(gm, both).T.astype(BF)

    def chunk(c, carry):
        rows = pl.ds(pl.multiple_of(c * ROWS, ROWS), ROWS)
        for half in range(2):
            for j in range(KEYS // LANES):
                at = slice(j * LANES, (j + 1) * LANES)
                ds_ref[half, rows, at] = (
                    e_ref[half, rows, at].astype(F32) * dp_scr[half, rows, at]
                ).astype(BF)
        return carry

    lax.fori_loop(0, frames // ROWS, chunk, 0)
    dk_t = dot_tn(jnp.concatenate(qus, axis=0), ds_ref[...].reshape(2 * frames, KEYS))
    dk_ref[...] = dk_t.T.astype(BF)


def pairs_call(kernel, name, ins, outs, scratch, flops):
    pairs = ins[0][0].shape[1] // LANES

    def spec(shape, rows):
        if rows:
            return pl.BlockSpec((rows, LANES), lambda i: (0, i))
        return pl.BlockSpec((2, *shape[1:]), lambda i: (i, 0, 0))

    moved = sum(math.prod(a.shape) * a.dtype.itemsize for a, _ in ins)
    moved += sum(math.prod(shape) * jnp.dtype(dtype).itemsize for shape, dtype, _ in outs)
    return pl.pallas_call(
        kernel,
        grid=(pairs,),
        in_specs=[spec(a.shape, rows) for a, rows in ins],
        out_specs=[spec(shape, rows) for shape, _, rows in outs],
        out_shape=[jax.ShapeDtypeStruct(shape, dtype) for shape, dtype, _ in outs],
        scratch_shapes=[pltpu.VMEM(shape, dtype) for shape, dtype in scratch],
        compiler_params=pltpu.CompilerParams(vmem_limit_bytes=56 * 1024 * 1024),
        cost_estimate=pl.CostEstimate(
            flops=16 * flops * pairs, bytes_accessed=moved, transcendentals=0
        ),
        name=name,
    )(*[a for a, _ in ins])


def keys_back(q, v, u, grad, mixed, inverse, weights):
    frames, width = q.shape
    return pairs_call(
        keys_back_kernel,
        "keys_back",
        [
            (q, frames),
            (v, KEYS),
            (u, 1),
            (grad, frames),
            (mixed, frames),
            (inverse, frames),
            (weights, 0),
        ],
        [
            ((width // HEAD_DIM, frames, KEYS), BF, 0),
            ((KEYS, width), BF, KEYS),
            ((KEYS, width), BF, KEYS),
        ],
        [((2, frames, KEYS), F32)],
        3 * frames * KEYS * LANES,
    )


def unskew(ds_ref, dun_scr, half, c):
    first = (BLOCK // ROWS - 1 - c) * LANES
    for pair in range(ROWS // 16):
        rows = pl.ds(pl.multiple_of(c * ROWS + 16 * pair, 16), 16)
        before = [jnp.zeros((8, LANES), F32)] * 2
        for j in range(WINDOW // LANES):
            outs = []
            if j < KEYS // LANES:
                scores = ds_ref[half, rows, j * LANES : (j + 1) * LANES].astype(F32)
            for part in range(2):
                near, far, upper, lane = tile_cut(2 * pair + part)
                if j < KEYS // LANES:
                    score = scores[8 * part : 8 * part + 8]
                    moved = jnp.where(
                        upper,
                        pltpu.roll(score, near, 1),
                        pltpu.roll(score, far, 1) if far else score,
                    )
                else:
                    moved = jnp.zeros((8, LANES), F32)
                outs.append(jnp.where(lane >= jnp.where(upper, near, far), moved, before[part]))
                before[part] = moved
            there = pl.ds(pl.multiple_of(first + j * LANES, LANES), LANES)
            dun_scr[rows, there] = jnp.concatenate(outs, axis=0).astype(BF)


def queries_back_kernel(
    q_ref, k_ref, r_ref, b_ref, ds_ref, dq_ref, dr_ref, du_ref, db_ref,
    dun0_scr, dun1_scr, r_scr, rc_scr, dqk_scr, wide_scr, four_scr,
):
    scale = HEAD_DIM**-0.5
    frames = q_ref.shape[0]
    duns = (dun0_scr, dun1_scr)
    part = RELS // (BLOCK // ROWS)

    @pl.when(pl.program_id(0) == 0)
    def _():
        dun0_scr[...] = jnp.zeros_like(dun0_scr)
        dun1_scr[...] = jnp.zeros_like(dun1_scr)

    qb = (q_ref[...].astype(F32) + b_ref[...].astype(F32)) * scale
    qbs = [slotted(twice(qb, own_lanes(half))) for half in range(2)]
    rc_scr[...] = four_rows(r_ref, r_scr, own_lanes(0))
    k = k_ref[...]

    def relative_products(half, c):
        rows = pl.ds(pl.multiple_of(c * ROWS, ROWS), ROWS)
        wide_scr[rows, :] = dot(duns[half][rows, :], rc_scr[...])
        lanes = pl.ds(pl.multiple_of(c * part, part), part)
        four_scr[:, lanes] = dot_tn(qbs[half], duns[half][:, lanes])

    def first_head(c, carry):
        rows = pl.ds(pl.multiple_of(c * ROWS, ROWS), ROWS)
        unskew(ds_ref, dun0_scr, 0, c)
        for half in range(2):
            dqk_scr[half, rows, :] = dot(ds_ref[half, rows, :], k)
        return carry

    def second_head(c, carry):
        unskew(ds_ref, dun1_scr, 1, c)
        relative_products(0, c)
        return carry

    def finish(half):
        own = own_lanes(half)
        wide = wide_scr[...] * scale
        slot = lax.broadcasted_iota(jnp.int32, (frames, LANES), 1) // HEAD_DIM
        place = 3 - lax.broadcasted_iota(jnp.int32, (frames, LANES), 0) % 4
        picked = jnp.where(slot == place, wide[:, :LANES], 0.0)
        picked += jnp.where(slot + 2 == place, wide[:, LANES:], 0.0)
        dq_r = jnp.where(own, picked + pltpu.roll(picked, HEAD_DIM, 1), 0.0)
        dq_k = jnp.where(own, dqk_scr[half] * scale, 0.0)
        four = four_scr[...]
        dr_t = four[:HEAD_DIM]
        for s in (1, 2, 3):
            dr_t += pltpu.roll(four[s * HEAD_DIM : (s + 1) * HEAD_DIM], s, 1)
        return dq_k, dq_r, dr_t

    lax.fori_loop(0, frames // ROWS, first_head, 0)
    lax.fori_loop(0, frames // ROWS, second_head, 0)
    dq_k0, dq_r0, dr_t0 = finish(0)
    rc_scr[...] = four_rows(r_ref, r_scr, own_lanes(1))
    wide_scr[...] = dot(dun1_scr[...], rc_scr[...])
    four_scr[...] = dot_tn(qbs[1], dun1_scr[...])
    dq_k1, dq_r1, dr_t1 = finish(1)
    dq_k, dq_r = dq_k0 + dq_k1, dq_r0 + dq_r1
    dq_ref[...] = (dq_k + dq_r).astype(BF)
    du_ref[...] = jnp.sum(dq_k, axis=0, keepdims=True)
    db_ref[...] = jnp.sum(dq_r, axis=0, keepdims=True)
    dr_ref[...] = jnp.concatenate([dr_t0, dr_t1], axis=0).T.astype(BF)


def queries_back(q, k, rel, b, scores):
    frames, width = q.shape
    return pairs_call(
        queries_back_kernel,
        "queries_back",
        [(q, frames), (k, KEYS), (rel, RELS), (b, 1), (scores, 0)],
        [
            ((frames, width), BF, frames),
            ((RELS, width), BF, RELS),
            ((1, width), F32, 1),
            ((1, width), F32, 1),
        ],
        [
            ((frames, RELS), BF),
            ((frames, RELS), BF),
            ((RELS + 8, LANES), F32),
            ((RELS, 2 * LANES), BF),
            ((2, frames, LANES), F32),
            ((frames, 2 * LANES), F32),
            ((2 * LANES, RELS), F32),
        ],
        frames * LANES * (KEYS + 2 * RELS),
    )


MESH = pl.DeviceIdType.MESH


def grid_of(items, seq):
    side = math.isqrt(items)
    return side, seq // 2


def whereabouts(side):
    item, place = lax.axis_index("items"), lax.axis_index("seq")
    return item // side, item % side, place // 2, place % 2


def at_device(side, y, x, z, core):
    return (y * side + x, z * 2 + core)


def meet(partners):
    barrier = pltpu.get_barrier_semaphore()
    for partner in partners:
        pl.semaphore_signal(barrier, inc=1, device_id=partner, device_id_type=MESH)
    pl.semaphore_wait(barrier, len(partners))


def all_partners(side, depth, y, x, z, core):
    return (
        [at_device(side, y, x, z, 1 - core)]
        + [at_device(side, y, (x + d) % side, z, core) for d in range(1, side)]
        + [at_device(side, (y + d) % side, x, z, core) for d in range(1, side)]
        + [at_device(side, y, x, (z + d) % depth, core) for d in range(1, depth)]
    )


def send(source, target, send_sem, recv_sem, device):
    copy = pltpu.make_async_remote_copy(
        src_ref=source, dst_ref=target, send_sem=send_sem, recv_sem=recv_sem,
        device_id=device, device_id_type=MESH,
    )
    copy.start()
    return copy


AHEAD = 4
LAG = 2


def gather_order(p):
    if p % 8 == 4:
        return "yxz" if p % 16 == 4 else "xyz"
    return "zxy" if p % 2 else "zyx"


def gather_kernel(side, depth, pieces, count, *refs):
    shards, outs = refs[:count], refs[count : 2 * count]
    own_sem, s_sem, r_sem, cs_sem, cr_sem = refs[2 * count :]
    y, x, z, core = whereabouts(side)
    meet(all_partners(side, depth, y, x, z, core))
    owns = [
        pltpu.make_async_copy(shard, out.at[y, x, z, core], own_sem.at[i])
        for i, (shard, out) in enumerate(zip(shards, outs))
    ]
    for own in owns:
        own.start()
    copies = {}

    def region(p, done):
        i, cols = pieces[p]
        every = slice(None)
        return outs[i].at[
            every if "y" in done else y,
            every if "x" in done else x,
            every if "z" in done else z,
            core, :, cols,
        ]

    def start(p, k):
        order = gather_order(p)
        axis = order[k]
        here = region(p, order[:k])
        i, cols = pieces[p]
        copies[p, k] = [
            send(
                here if k else shards[i].at[:, cols], here,
                s_sem.at[k, p, d - 1], r_sem.at[k, p, d - 1],
                at_device(
                    side,
                    (y + d) % side if axis == "y" else y,
                    (x + d) % side if axis == "x" else x,
                    (z + d) % depth if axis == "z" else z,
                    core,
                ),
            )
            for d in range(1, depth if axis == "z" else side)
        ]

    def arrived(p, k):
        for copy in copies[p, k]:
            copy.wait_recv()

    for p in range(min(AHEAD, len(pieces))):
        start(p, 0)
    for own in owns:
        own.wait()
    for t in range(len(pieces) + 3 * LAG):
        if t + AHEAD < len(pieces):
            start(t + AHEAD, 0)
        for k in (1, 2):
            p = t - (k - 1) * LAG
            if 0 <= p < len(pieces):
                arrived(p, k - 1)
                start(p, k)
        p = t - 2 * LAG
        if 0 <= p < len(pieces):
            arrived(p, 2)
            here = region(p, "yxz")
            copies[p, 3] = [
                send(here, here, cs_sem.at[p], cr_sem.at[p], at_device(side, y, x, z, 1 - core))
            ]
        p = t - 3 * LAG
        if 0 <= p < len(pieces):
            arrived(p, 3)
    for started in copies.values():
        for copy in started:
            copy.wait_send()


def gather_by_kernel(shards, side, depth):
    pieces = [
        (i, pl.ds(c, min(512, shard.shape[1])))
        for i, shard in enumerate(shards)
        for c in range(0, shard.shape[1], 512)
    ]
    dma = pltpu.SemaphoreType.DMA
    n = len(pieces)
    outs = pl.pallas_call(
        functools.partial(gather_kernel, side, depth, pieces, len(shards)),
        in_specs=[pl.BlockSpec(memory_space=pl.ANY)] * len(shards),
        out_specs=[pl.BlockSpec(memory_space=pl.ANY)] * len(shards),
        out_shape=[
            jax.ShapeDtypeStruct((side, side, depth, 2, *shard.shape), shard.dtype)
            for shard in shards
        ],
        scratch_shapes=[dma((len(shards),))]
        + [dma((3, n, max(side, depth) - 1))] * 2
        + [dma((n,))] * 2,
        compiler_params=pltpu.CompilerParams(
            collective_id=1, has_side_effects=True, vmem_limit_bytes=48 * 1024 * 1024
        ),
        name="gather",
    )(*shards)
    return [out.reshape(-1, out.shape[-1]) for out in outs]


def put_block(out_ref, piece, total):
    rows = total.shape[0]
    lane = lax.broadcasted_iota(jnp.int32, (rows, LANES), 1)
    each = LANES // 4
    for tile in range(total.shape[1] // LANES):
        some = total[:, tile * LANES : (tile + 1) * LANES]
        for q in range(4):
            turn = (each * (piece - q)) % LANES
            moved = pltpu.roll(some, turn, 1) if turn else some
            at = slice((4 * tile + q) * LANES, (4 * tile + q + 1) * LANES)
            rest = out_ref[:, at] if piece else jnp.zeros_like(some)
            out_ref[:, at] = jnp.where(lane // each == piece, moved, rest)


Z_FIRST = (6, 12)


def added(parts):
    if len(parts) == 2:
        return parts[0] + parts[1]
    return sum(part.astype(F32) for part in parts).astype(BF)


def scatter_kernel(side, depth, pieces, count, *refs):
    ops, (small_out, four_out, in_out, out_out) = refs[:count], refs[count : count + 4]
    l_buf, r_buf, sum_buf, g_buf, c_buf, a_buf, b_buf, z_buf = refs[count + 4 : count + 12]
    e_buf, f_buf, h_buf = refs[count + 12 : count + 15]
    l_sem, r_sem, cs_sem, cr_sem, as_sem, ar_sem, bs_sem, br_sem, zs_sem, zr_sem = refs[count + 15 :]
    y, x, z, core = whereabouts(side)
    rows, wide = g_buf.shape[-2:]
    section = depth * 2 * rows
    last = len(pieces)
    meet(all_partners(side, depth, y, x, z, core))

    def cols(p):
        return pl.ds(0, pieces[p][5])

    def z_first(p):
        return Z_FIRST.index(p) if p in Z_FIRST else None

    most = l_buf.shape[1]
    chunks = []
    for p, (left, *_) in enumerate(pieces):
        deep = most if left is None else ops[left].shape[0]
        chunks += [(p, k, min(most, deep - k)) for k in range(0, deep, most)]

    def load(s):
        p, k, many = chunks[s]
        left, left_at, right, right_at, place, many_cols = pieces[p]
        slot = s % 2
        if left is None:
            copies = [
                pltpu.make_async_copy(
                    ops[right], g_buf.at[p % 2, :, :, :, :, :, cols(p)], r_sem.at[slot]
                )
            ]
        else:
            copies = [
                pltpu.make_async_copy(
                    ops[left].at[pl.ds(k, many), pl.ds(left_at, wide)],
                    l_buf.at[slot, pl.ds(0, many)], l_sem.at[slot],
                ),
                pltpu.make_async_copy(
                    ops[right].at[pl.ds(k, many), pl.ds(right_at, many_cols)],
                    r_buf.at[slot, pl.ds(0, many), cols(p)], r_sem.at[slot],
                ),
            ]
        for copy in copies:
            copy.start()
        return copies

    def multiply(s):
        p, k, many = chunks[s]
        slot = s % 2
        first, final = k == 0, k + many == ops[pieces[p][0]].shape[0]

        def section_product(i, carry):
            lanes = pl.ds(pl.multiple_of(i * section, section), section)
            total = dot_tn(l_buf[slot, 0:many, lanes], r_buf[slot, 0:many, cols(p)])
            if not first:
                total += sum_buf[lanes, cols(p)]
            if final:
                total = total.astype(BF).reshape(depth, 2, rows, pieces[p][5])
                g_buf[p % 2, i // side, i % side, :, :, :, cols(p)] = total
            else:
                sum_buf[lanes, cols(p)] = total
            return carry

        lax.fori_loop(0, side * side, section_product, 0)

    c_copies, a_copies, b_copies, z_copies = [], [], [], []
    loads = [load(0)]
    for t in range(last + 1 + 3 * LAG):
        p = t
        if p < last:
            if p >= 2:
                c_copies[p - 2].wait_send()
            for s in [s for s in range(len(chunks)) if chunks[s][0] == p]:
                if s + 1 < len(chunks):
                    loads.append(load(s + 1))
                for copy in loads[s]:
                    copy.wait()
                if pieces[p][0] is not None:
                    multiply(s)
            c_copies.append(
                send(
                    g_buf.at[p % 2, :, :, :, 1 - core, :, cols(p)],
                    c_buf.at[p, :, :, :, :, cols(p)],
                    cs_sem.at[p], cr_sem.at[p], at_device(side, y, x, z, 1 - core),
                )
            )
        p = t - 1
        if 0 <= p < last:
            c_copies[p].wait_recv()

            def add_core(i, carry, p=p):
                at = (i // side, i % side)
                c_buf[p, *at, :, :, cols(p)] += g_buf[p % 2, *at, :, core, :, cols(p)]
                return carry

            lax.fori_loop(0, side * side, add_core, 0)
            a_copies.append(
                [
                    send(
                        c_buf.at[p, :, :, (z + d) % depth, :, cols(p)],
                        e_buf.at[z_first(p), d - 1, :, :, :, cols(p)],
                        as_sem.at[p, d - 1], ar_sem.at[p, d - 1],
                        at_device(side, y, x, (z + d) % depth, core),
                    )
                    for d in range(1, depth)
                ]
                if z_first(p) is not None
                else [
                    send(
                        c_buf.at[p, (y + d) % side, :, :, :, cols(p)]
                        if p % 2
                        else c_buf.at[p, :, (x + d) % side, :, :, cols(p)],
                        a_buf.at[p, d - 1, :, :, :, cols(p)],
                        as_sem.at[p, d - 1], ar_sem.at[p, d - 1],
                        at_device(side, (y + d) % side, x, z, core)
                        if p % 2
                        else at_device(side, y, (x + d) % side, z, core),
                    )
                    for d in range(1, side)
                ]
            )
        p = t - 1 - LAG
        if 0 <= p < last:
            for copy in a_copies[p]:
                copy.wait_recv()

            def add_first(j, carry, p=p):
                own = c_buf[p, y, j, :, :, cols(p)] if p % 2 else c_buf[p, j, x, :, :, cols(p)]
                a_buf[p, 0, j, :, :, cols(p)] = added(
                    [own] + [a_buf[p, d, j, :, :, cols(p)] for d in range(side - 1)]
                )
                return carry

            q = z_first(p)
            if q is None:
                lax.fori_loop(0, side, add_first, 0)
            else:
                for j in range(side):
                    e_buf[q, 0, j, :, :, cols(p)] = added(
                        [c_buf[p, j, :, z, :, cols(p)]]
                        + [e_buf[q, d, j, :, :, cols(p)] for d in range(depth - 1)]
                    )
            b_copies.append(
                [
                    send(
                        e_buf.at[q, 0, :, (x + d) % side, :, cols(p)],
                        f_buf.at[q, d - 1, :, :, cols(p)],
                        bs_sem.at[p, d - 1], br_sem.at[p, d - 1],
                        at_device(side, y, (x + d) % side, z, core),
                    )
                    for d in range(1, side)
                ]
                if q is not None
                else [
                    send(
                        a_buf.at[p, 0, ((x if p % 2 else y) + d) % side, :, :, cols(p)],
                        b_buf.at[p, d - 1, :, :, cols(p)],
                        bs_sem.at[p, d - 1], br_sem.at[p, d - 1],
                        at_device(side, y, (x + d) % side, z, core)
                        if p % 2
                        else at_device(side, (y + d) % side, x, z, core),
                    )
                    for d in range(1, side)
                ]
            )
        p = t - 1 - 2 * LAG
        if 0 <= p < last:
            for copy in b_copies[p]:
                copy.wait_recv()

            q = z_first(p)
            if q is None:
                own = a_buf[p, 0, x if p % 2 else y, :, :, cols(p)]
                b_buf[p, 0, :, :, cols(p)] = added(
                    [own] + [b_buf[p, d, :, :, cols(p)] for d in range(side - 1)]
                )
            else:
                f_buf[q, 0, :, :, cols(p)] = added(
                    [e_buf[q, 0, :, x, :, cols(p)]]
                    + [f_buf[q, d, :, :, cols(p)] for d in range(side - 1)]
                )
            z_copies.append(
                [
                    send(
                        f_buf.at[q, 0, (y + d) % side, :, cols(p)],
                        h_buf.at[q, d - 1, :, cols(p)],
                        zs_sem.at[p, d - 1], zr_sem.at[p, d - 1],
                        at_device(side, (y + d) % side, x, z, core),
                    )
                    for d in range(1, side)
                ]
                if q is not None
                else [
                    send(
                        b_buf.at[p, 0, (z + d) % depth, :, cols(p)],
                        z_buf.at[p, d - 1, :, cols(p)],
                        zs_sem.at[p, d - 1], zr_sem.at[p, d - 1],
                        at_device(side, y, x, (z + d) % depth, core),
                    )
                    for d in range(1, depth)
                ]
            )
        p = t - 1 - 3 * LAG
        if 0 <= p < last:
            for copy in z_copies[p]:
                copy.wait_recv()
            q = z_first(p)
            total = (b_buf[p, 0, z, :, cols(p)] if q is None else f_buf[q, 0, y, :, cols(p)]).astype(F32)
            for d in range(depth - 1 if q is None else side - 1):
                total += (z_buf[p, d, :, cols(p)] if q is None else h_buf[q, d, :, cols(p)]).astype(F32)
            kind, index = pieces[p][4]
            if kind == 0:
                small_out[...] = total
            elif kind == 1:
                four_out[index] = total
            elif kind == 2:
                put_block(in_out, index, total)
            else:
                at = pieces[p][3]
                out_out[index * rows : (index + 1) * rows, at : at + pieces[p][5]] = total
    for p in range(last):
        for copy in ([c_copies[p]] if p >= last - 2 else []) + a_copies[p] + b_copies[p] + z_copies[p]:
            copy.wait_send()


def scatter_by_kernel(pairs, before, active, hidden, low, small, side, depth):
    width = low.shape[1]
    rows = width // (side * side * depth * 2)
    ops, pieces = [], []

    def operand(array):
        ops.append(array)
        return len(ops) - 1

    slabs = small.reshape(side, side, depth, 2, rows, small.shape[1])
    pieces.append((None, 0, operand(slabs), 0, (0, 0), small.shape[1]))
    seen, many = {}, 0
    for left, right in pairs:
        if id(left) not in seen:
            seen[id(left)] = operand(left)
        at_right = operand(right)
        for c in range(0, right.shape[1], width):
            pieces.append((seen[id(left)], 0, at_right, c, (1, many), width))
            many += 1
    at_hidden, at_before = operand(hidden), operand(before)
    at_active, at_low = operand(active), operand(low)
    steps = range(before.shape[1] // width)
    pieces += [(at_hidden, 0, at_before, c * width, (2, c), width) for c in steps]
    pieces += [(at_active, c * width, at_low, 0, (3, c), width) for c in steps]
    last = pieces.pop()
    pieces += [(*last[:3], at, last[4], width // 2) for at in (0, width // 2)]
    n = len(pieces)
    dma = pltpu.SemaphoreType.DMA
    outs = (
        (rows, small.shape[1]),
        (many, rows, width),
        (rows, before.shape[1]),
        (rows * len(steps), width),
    )
    return pl.pallas_call(
        functools.partial(scatter_kernel, side, depth, pieces, len(ops)),
        in_specs=[pl.BlockSpec(memory_space=pl.ANY)] * len(ops),
        out_specs=[pl.BlockSpec(memory_space=pltpu.VMEM)] * len(outs),
        out_shape=[jax.ShapeDtypeStruct(shape, F32) for shape in outs],
        scratch_shapes=[
            pltpu.VMEM((2, width, width), BF),
            pltpu.VMEM((2, width, width), BF),
            pltpu.VMEM((width, width), F32),
            pltpu.VMEM((2, side, side, depth, 2, rows, width), BF),
            pltpu.VMEM((n, side, side, depth, rows, width), BF),
            pltpu.VMEM((n, side - 1, side, depth, rows, width), BF),
            pltpu.VMEM((n, side - 1, depth, rows, width), BF),
            pltpu.VMEM((n, depth - 1, rows, width), BF),
            pltpu.VMEM((len(Z_FIRST), depth - 1, side, side, rows, width), BF),
            pltpu.VMEM((len(Z_FIRST), side - 1, side, rows, width), BF),
            pltpu.VMEM((len(Z_FIRST), side - 1, rows, width), BF),
            dma((2,)),
            dma((2,)),
            dma((n,)),
            dma((n,)),
        ]
        + [dma((n, max(side, depth) - 1))] * 6,
        compiler_params=pltpu.CompilerParams(
            collective_id=2, has_side_effects=True, vmem_limit_bytes=58 * 1024 * 1024
        ),
        name="scatter",
    )(*ops)


def products_kernel(ranges, *refs):
    p = pl.program_id(0)
    out_ref = refs[-1]
    section = 512
    for i, (first, count) in enumerate(ranges):
        left_ref, right_ref = refs[2 * i], refs[2 * i + 1]

        @pl.when((p >= first) & (p < first + count))
        def _(left_ref=left_ref, right_ref=right_ref):
            def part(j, carry):
                some = pl.ds(pl.multiple_of(j * section, section), section)
                out_ref[some, :] = dot_tn(left_ref[:, some], right_ref[...]).astype(BF)
                return carry

            lax.fori_loop(0, out_ref.shape[0] // section, part, 0)


def products(pairs):
    frames, width = pairs[0][0].shape
    specs, ops, ranges, first = [], [], [], 0
    for left, right in pairs:
        count = max(left.shape[1], right.shape[1]) // width
        for array in (left, right):
            most = array.shape[1] // width - 1
            specs.append(
                pl.BlockSpec(
                    (frames, width), lambda p, first=first, most=most: (0, jnp.clip(p - first, 0, most))
                )
            )
            ops.append(array)
        ranges.append((first, count))
        first += count
    return pl.pallas_call(
        functools.partial(products_kernel, ranges),
        grid=(first,),
        in_specs=specs,
        out_specs=pl.BlockSpec((width, width), lambda p: (0, p)),
        out_shape=jax.ShapeDtypeStruct((width, first * width), BF),
        compiler_params=pltpu.CompilerParams(vmem_limit_bytes=48 * 1024 * 1024),
        cost_estimate=pl.CostEstimate(
            flops=2 * frames * width * width * first,
            bytes_accessed=(3 * frames + 2 * width) * width * first,
            transcendentals=0,
        ),
        name="products",
    )(*ops)


def by_kernel(rows):
    items, seq = lax.axis_size("items"), lax.axis_size("seq")
    return rows % 16 == 0 and math.isqrt(items) ** 2 == items and items > 1 and seq > 2 and seq % 2 == 0


def norm(values):
    center = values - jnp.mean(values, axis=-1, keepdims=True)
    spread = jnp.mean(center * center, axis=-1, keepdims=True)
    scale = lax.rsqrt(spread + EPSILON)
    return center * scale, scale


def norm_back(grad, unit, scale, gain):
    inner = grad * gain
    mean_inner = jnp.mean(inner, axis=-1, keepdims=True)
    mean_both = jnp.mean(inner * unit, axis=-1, keepdims=True)
    return scale * (inner - mean_inner - unit * mean_both), jnp.sum(grad * unit, axis=0)


def silu_slope(value):
    s = jax.nn.sigmoid(value)
    return s * (1.0 + value * (1.0 - s))


def pack_in(shard, count):
    rows, hidden = shard.shape
    pieces = hidden // count // rows
    if 4 * rows == LANES and pieces == 4:
        return reorder(shard, True, shard.dtype)
    return shard.reshape(rows, count, pieces, rows).transpose(0, 2, 1, 3).reshape(rows, hidden)


def unpack_in(shard, count):
    rows, hidden = shard.shape
    pieces = hidden // count // rows
    if 4 * rows == LANES and pieces == 4:
        return reorder(shard, False, F32)
    return shard.reshape(rows, pieces, count, rows).transpose(0, 2, 1, 3).reshape(rows, hidden)


def pack_out(shard, rows):
    pieces, width = shard.shape[0] // rows, shard.shape[1]
    return shard.reshape(pieces, rows, width).transpose(1, 0, 2).reshape(rows, pieces * width)


def unpack_out(shard, width):
    rows, pieces = shard.shape[0], shard.shape[1] // width
    return shard.reshape(rows, pieces, width).transpose(1, 0, 2).reshape(rows * pieces, width)


def reorder_kernel(to_pieces, in_ref, out_ref):
    each = LANES // 4
    tiles = in_ref.shape[1] // LANES // 4
    lane = lax.broadcasted_iota(jnp.int32, (in_ref.shape[0], LANES), 1)

    def tile(at):
        return in_ref[:, at * LANES : (at + 1) * LANES].astype(F32)

    for k in range(tiles):
        for c in range(4):
            total = None
            for q in range(4):
                some = tile(4 * k + q) if to_pieces else tile(q * tiles + k)
                turn = each * (q - c) % LANES
                some = pltpu.roll(some, turn, 1) if turn else some
                total = some if total is None else jnp.where(lane // each == q, some, total)
            at = (c * tiles + k) if to_pieces else (4 * k + c)
            out_ref[:, at * LANES : (at + 1) * LANES] = total.astype(out_ref.dtype)


def reorder(shard, to_pieces, dtype):
    return pl.pallas_call(
        functools.partial(reorder_kernel, to_pieces),
        out_shape=jax.ShapeDtypeStruct(shard.shape, dtype),
        name="reorder",
    )(shard)


def halves(size):
    return [pl.ds(0, size // 2), pl.ds(size // 2, size // 2)]


def feed_forward_kernel(hid_ref, in_ref, out_w_ref, active_ref, slope_ref, out_ref):
    @pl.when(pl.program_id(0) == 0)
    def _():
        out_ref[...] = jnp.zeros_like(out_ref)

    parts = halves(in_ref.shape[1])
    befores = [dot(hid_ref[...], in_ref[:, at]) for at in parts]
    actives = []
    for at, before in zip(parts, befores):
        gate = jax.nn.sigmoid(before)
        active = (before * gate).astype(BF)
        active_ref[:, at] = active
        slope_ref[:, at] = (gate * (1.0 + before * (1.0 - gate))).astype(BF)
        actives.append(active)
    out_ref[...] += sum(dot(active, out_w_ref[at, :]) for at, active in zip(parts, actives))


def feed_forward_back_kernel(low_ref, in_ref, out_w_ref, slope_ref, before_ref, hid_ref):
    @pl.when(pl.program_id(0) == 0)
    def _():
        hid_ref[...] = jnp.zeros_like(hid_ref)

    parts = halves(in_ref.shape[1])
    actives = [dot_nt(low_ref[...], out_w_ref[at, :]) for at in parts]
    befores = []
    for at, active in zip(parts, actives):
        before = (active * slope_ref[:, at].astype(F32)).astype(BF)
        before_ref[:, at] = before
        befores.append(before)
    hid_ref[...] += sum(dot_nt(before, in_ref[:, at]) for at, before in zip(parts, befores))


def hidden_blocks(frames, width, hidden_width):
    step = width // 2
    per = width // step
    return (
        hidden_width // step,
        pl.BlockSpec((frames, width), lambda j: (0, 0)),
        pl.BlockSpec((width, step), lambda j: (0, j)),
        pl.BlockSpec((step, width), lambda j: (j % per, j // per)),
        pl.BlockSpec((frames, step), lambda j: (0, j)),
    )


def feed_forward(hidden, weight_in, weight_out):
    frames, width = hidden.shape
    hidden_width = weight_in.shape[1]
    steps, whole, in_block, out_block, unit_block = hidden_blocks(frames, width, hidden_width)
    units = jax.ShapeDtypeStruct((frames, hidden_width), BF)
    return pl.pallas_call(
        feed_forward_kernel,
        grid=(steps,),
        in_specs=[whole, in_block, out_block],
        out_specs=[unit_block, unit_block, whole],
        out_shape=[units, units, jax.ShapeDtypeStruct((frames, width), F32)],
        compiler_params=pltpu.CompilerParams(vmem_limit_bytes=48 * 1024 * 1024),
        cost_estimate=pl.CostEstimate(
            flops=4 * frames * width * hidden_width,
            bytes_accessed=4 * (width + frames) * hidden_width,
            transcendentals=frames * hidden_width,
        ),
        name="feed_forward",
    )(hidden, weight_in, weight_out)


def feed_forward_back(grad, slope, weight_in, weight_out):
    frames, width = grad.shape
    hidden_width = weight_in.shape[1]
    low = (0.5 * grad).astype(BF)
    steps, whole, in_block, out_block, unit_block = hidden_blocks(frames, width, hidden_width)
    before, hid = pl.pallas_call(
        feed_forward_back_kernel,
        grid=(steps,),
        in_specs=[whole, in_block, out_block, unit_block],
        out_specs=[unit_block, whole],
        out_shape=[
            jax.ShapeDtypeStruct((frames, hidden_width), BF),
            jax.ShapeDtypeStruct((frames, width), F32),
        ],
        compiler_params=pltpu.CompilerParams(vmem_limit_bytes=48 * 1024 * 1024),
        cost_estimate=pl.CostEstimate(
            flops=4 * frames * width * hidden_width,
            bytes_accessed=4 * (width + frames) * hidden_width,
            transcendentals=0,
        ),
        name="feed_forward_back",
    )(low, weight_in, weight_out, slope)
    return hid, before, low


def depthwise_kernel(wide_ref, taps_ref, out_ref):
    step = 64
    for first in range(0, out_ref.shape[0], step):
        total = jnp.zeros((step, LANES), F32)
        for k in range(TAPS):
            total += taps_ref[k : k + 1, :] * wide_ref[first + k : first + k + step, :]
        out_ref[first : first + step, :] = total


def depthwise(wide, taps):
    rows, width = wide.shape
    column = lambda rows: pl.BlockSpec((rows, LANES), lambda i: (0, i))
    return pl.pallas_call(
        depthwise_kernel,
        grid=(width // LANES,),
        in_specs=[column(rows), column(TAPS)],
        out_specs=column(rows - 2 * HALF),
        out_shape=jax.ShapeDtypeStruct((rows - 2 * HALF, width), F32),
        cost_estimate=pl.CostEstimate(
            flops=2 * rows * width * TAPS, bytes_accessed=8 * rows * width, transcendentals=0
        ),
        name="depthwise",
    )(wide, taps)


def depthwise_back_kernel(wide_ref, grad_ref, taps_ref, out_ref, dtaps_ref):
    step = 64
    frames = out_ref.shape[0]
    for first in range(0, frames, step):
        total = jnp.zeros((step, LANES), F32)
        for k in range(TAPS):
            at = first + 2 * HALF - k
            total += taps_ref[k : k + 1, :] * grad_ref[at : at + step, :]
        out_ref[first : first + step, :] = total
    sums = [jnp.zeros((8, LANES), F32)] * TAPS
    for first in range(0, frames, 8):
        grad = grad_ref[first + HALF : first + HALF + 8, :]
        sums = [sums[k] + grad * wide_ref[first + k : first + k + 8, :] for k in range(TAPS)]
    for k in range(TAPS):
        dtaps_ref[k : k + 1, :] = jnp.sum(sums[k], axis=0, keepdims=True)


def depthwise_back(wide, grad, taps):
    rows, width = wide.shape
    frames = rows - 2 * HALF
    column = lambda rows: pl.BlockSpec((rows, LANES), lambda i: (0, i))
    return pl.pallas_call(
        depthwise_back_kernel,
        grid=(width // LANES,),
        in_specs=[column(rows), column(rows), column(TAPS)],
        out_specs=[column(frames), column(TAPS)],
        out_shape=[
            jax.ShapeDtypeStruct((frames, width), F32),
            jax.ShapeDtypeStruct((TAPS, width), F32),
        ],
        cost_estimate=pl.CostEstimate(
            flops=4 * rows * width * TAPS, bytes_accessed=12 * rows * width, transcendentals=0
        ),
        name="depthwise_back",
    )(wide, grad, taps)


def shifted(values, by):
    size = lax.axis_size("seq")
    pairs = [(i, i + by) for i in range(size) if 0 <= i + by < size]
    return lax.ppermute(values, "seq", pairs)


def all_gather(shard):
    return lax.all_gather(shard, AXES, axis=0, tiled=True)


def gather_each(shards):
    if by_kernel(shards[0].shape[0]):
        side, depth = grid_of(lax.axis_size("items"), lax.axis_size("seq"))
        return gather_by_kernel(shards, side, depth)
    return [all_gather(shard) for shard in shards]


def scatter_sum(grads):
    return lax.psum_scatter(grads, AXES, scatter_dimension=0, tiled=True)


def scatter_each(pairs, before, active, hidden, low, small):
    count = lax.axis_size("items") * lax.axis_size("seq")
    width = low.shape[1]
    rows = width // count
    if by_kernel(rows):
        side, depth = grid_of(lax.axis_size("items"), lax.axis_size("seq"))
        return scatter_by_kernel(pairs, before, active, hidden, low, small, side, depth)
    steps = range(0, before.shape[1], width)
    columns = [small] + [dot_tn(left, right).astype(BF) for left, right in pairs]
    many = sum(right.shape[1] for left, right in pairs)
    columns.append(dot_tn(hidden, before).astype(BF))
    columns += [dot_tn(active[:, c : c + width], low).astype(BF) for c in steps]
    total = scatter_sum(jnp.concatenate(columns, axis=1)).astype(F32)
    small, total = total[:, : small.shape[1]], total[:, small.shape[1] :]
    return (
        small,
        [total[:, i : i + width] for i in range(0, many, width)],
        unpack_in(total[:, many : many + before.shape[1]], count),
        unpack_out(total[:, many + before.shape[1] :], width),
    )


def after(value, earlier):
    return value + jnp.minimum(jnp.abs(earlier[0, 0]), 0).astype(value.dtype)


def body(
    features, item_spans, item_lengths,
    ffn1_gain, ffn1_in, ffn1_out, att_gain, w_query, w_key, w_value, w_pos, u_bias, v_bias, w_out,
    conv_gain, conv_in, depth_kernel, inner_gain, conv_out, ffn2_gain, ffn2_in, ffn2_out, final_gain,
    cotangent,
):
    count = lax.axis_size("items") * lax.axis_size("seq")
    block = lax.axis_index("seq")
    frames, width = features.shape[1], features.shape[2]
    rows = w_query.shape[0]
    hidden_width = ffn1_in.shape[1]

    spans, lengths = item_spans[0], item_lengths[0]
    places = jnp.arange(spans.shape[0], dtype=jnp.int32)
    starts = lax.cummax(jnp.where(spans > 0, places, 0), axis=0)
    start = jnp.take(starts, block)
    live = jnp.take(lengths, start)
    place = block - start
    near_before = jnp.where((block > 0) & (jnp.take(starts, jnp.maximum(block - 1, 0)) == start), 1.0, 0.0)
    last = spans.shape[0] - 1
    near_after = jnp.where((block < last) & (jnp.take(starts, jnp.minimum(block + 1, last)) == start), 1.0, 0.0)
    live_mask = (place * BLOCK + jnp.arange(frames, dtype=jnp.int32) < live).astype(F32)[:, None]

    vectors = jnp.concatenate(
        [ffn1_gain, att_gain, u_bias, v_bias, conv_gain, inner_gain, ffn2_gain, final_gain]
    )
    small = jnp.concatenate([depth_kernel, vectors.reshape(8, rows)], axis=0)
    small = jnp.pad(small, ((0, SMALL - small.shape[0]), (0, 0))).T
    table, w1_in, w1_out, w_q, w_k, w_v, w_r = gather_each(
        [small, pack_in(ffn1_in, count), pack_out(ffn1_out, rows), w_query, w_key, w_value, w_pos]
    )
    set_two = all_gather(
        jnp.concatenate(
            [
                after(w_out, w_r), conv_in, conv_out,
                pack_in(ffn2_in, count), pack_out(ffn2_out, rows),
            ],
            axis=1,
        )
    )
    table = table.T.astype(F32)
    taps = table[:TAPS]
    g_ffn1, g_att, g_u, g_v, g_conv, g_inner, g_ffn2, g_final = (table[TAPS + i] for i in range(8))
    w_o = set_two[:, :width]
    c_in = set_two[:, width : 3 * width]
    c_out = set_two[:, 3 * width : 4 * width]
    w2_in = set_two[:, 4 * width : 4 * width + hidden_width]
    w2_out = set_two[:, 4 * width + hidden_width :]

    distance = (BLOCK - 1 + BLOCK * place - jnp.arange(RELS, dtype=jnp.int32)).astype(F32)
    frequency = 1.0 / 10000.0 ** (jnp.arange(0, width, 2).astype(F32) / width)
    angles = distance[:, None] * frequency[None, :]
    waves = jnp.concatenate([jnp.sin(angles), jnp.cos(angles)], axis=1).astype(BF)

    stream = features[0]
    unit1, scale1 = norm(stream)
    hid1 = (unit1 * g_ffn1).astype(BF)
    active1, slope1, out1 = feed_forward(hid1, w1_in, w1_out)
    first = stream + 0.5 * out1

    unit2, scale2 = norm(first)
    hid2 = (unit2 * g_att).astype(BF)
    nearby = [shifted(hid2, 2), shifted(hid2, 1), hid2, shifted(hid2, -1), shifted(hid2, -2)]
    queries = dot(hid2, w_q).astype(BF)
    relative = dot(waves, w_r).astype(BF)
    u_row, v_row = g_u[None].astype(BF), g_v[None].astype(BF)
    positional = relative_scores(queries, relative, v_row)
    key_hid = lax.dynamic_slice_in_dim(jnp.concatenate(nearby, axis=0), (2 - place) * BLOCK, KEYS, 0)
    keys = dot(key_hid, w_k).astype(BF)
    values = dot(key_hid, w_v).astype(BF)
    mixed, shares, inverses = attend(live.reshape(1), queries, keys, values, u_row, positional)
    second = first + dot(mixed, w_o)

    unit3, scale3 = norm(second)
    hid3 = (unit3 * g_conv).astype(BF)
    doubled = dot(hid3, c_in)
    linear, gate = doubled[:, :width], jax.nn.sigmoid(doubled[:, width:])
    glu = (linear * gate * live_mask).astype(BF)
    wide = jnp.concatenate(
        [
            shifted(glu[frames - HALF :], 1).astype(F32) * near_before,
            glu.astype(F32),
            shifted(glu[:HALF], -1).astype(F32) * near_after,
        ],
        axis=0,
    )
    depth = depthwise(wide, taps)
    unit4, scale4 = norm(depth)
    inner = unit4 * g_inner
    active4 = jax.nn.silu(inner).astype(BF)
    third = second + dot(active4, c_out)

    unit5, scale5 = norm(third)
    hid5 = (unit5 * g_ffn2).astype(BF)
    active5, slope5, out5 = feed_forward(hid5, w2_in, w2_out)
    fourth = third + 0.5 * out5
    unit6, scale6 = norm(fourth)
    layer_out = unit6 * g_final

    grad, d_final = norm_back(cotangent[0], unit6, scale6, g_final)
    d_hid5, d_before5, low5 = feed_forward_back(grad, slope5, w2_in, w2_out)
    d_third, d_ffn2 = norm_back(d_hid5, unit5, scale5, g_ffn2)
    grad = grad + d_third
    low4 = grad.astype(BF)
    packed, low4 = lax.optimization_barrier(
        (products([(hid5, d_before5), (active5, low5), (active4, low4)]), low4)
    )
    sum_one = scatter_sum(packed)

    d_active4 = dot_nt(low4, c_out)
    d_depth, d_inner = norm_back(d_active4 * silu_slope(inner), unit4, scale4, g_inner)
    d_depth = d_depth.astype(BF)
    d_wide = jnp.concatenate(
        [
            shifted(d_depth[frames - HALF :], 1).astype(F32) * near_before,
            d_depth.astype(F32),
            shifted(d_depth[:HALF], -1).astype(F32) * near_after,
        ],
        axis=0,
    )
    d_glu, d_taps = depthwise_back(wide, d_wide, taps)
    d_glu = d_glu * live_mask
    d_doubled = jnp.concatenate(
        [(d_glu * gate).astype(BF), (d_glu * linear * gate * (1.0 - gate)).astype(BF)], axis=1
    )
    d_second, d_conv = norm_back(dot_nt(d_doubled, c_in), unit3, scale3, g_conv)
    grad = grad + d_second

    low2 = grad.astype(BF)
    d_mixed = dot_nt(low2, w_o).astype(BF)
    d_scores, d_k, d_v = keys_back(queries, values, u_row, d_mixed, mixed, inverses, shares)
    d_near = dot_nt(d_k, w_k) + dot_nt(d_v, w_v)
    d_own = lax.dynamic_slice_in_dim(d_near, place * BLOCK, BLOCK, 0)
    d_all = lax.dynamic_update_slice_in_dim(
        jnp.zeros((5 * BLOCK, width), BF), d_near.astype(BF), (2 - place) * BLOCK, 0
    )
    returned = [
        shifted(d_all[(2 + by) * BLOCK : (3 + by) * BLOCK], by).astype(F32) for by in (-2, -1, 1, 2)
    ]
    d_q, d_r, d_u, d_b = queries_back(queries, keys, relative, v_row, d_scores)
    d_hid2 = dot_nt(d_q, w_q) + d_own + sum(returned)
    d_first, d_att = norm_back(d_hid2, unit2, scale2, g_att)
    grad = grad + d_first

    d_hid1, d_before1, low1 = feed_forward_back(grad, slope1, w1_in, w1_out)
    d_stream, d_ffn1 = norm_back(d_hid1, unit1, scale1, g_ffn1)
    input_grad = grad + d_stream

    vectors = jnp.stack([d_ffn1, d_att, d_u[0], d_b[0], d_conv, d_inner, d_ffn2, d_final], axis=0)
    small = jnp.concatenate([d_taps, vectors], axis=0)
    small = jnp.pad(small, ((0, SMALL - small.shape[0]), (0, 0))).T.astype(BF)
    small, input_grad = lax.optimization_barrier((small, input_grad))
    g_small, many, g1_in, g1_out = scatter_each(
        [
            (mixed, low2), (hid3, d_doubled),
            (hid2, d_q), (key_hid, d_k), (key_hid, d_v), (waves, d_r),
        ],
        d_before1, active1, hid1, low1, small,
    )

    sum_one = sum_one.astype(F32)
    w = width
    h = hidden_width
    gains = [g_small[:, TAPS + i] for i in range(8)]
    return (
        layer_out[None],
        input_grad[None],
        gains[0],
        g1_in,
        g1_out,
        gains[1],
        many[3],
        many[4],
        many[5],
        many[6],
        gains[2],
        gains[3],
        many[0],
        gains[4],
        jnp.concatenate([many[1], many[2]], axis=1),
        g_small[:, :TAPS].T,
        gains[5],
        sum_one[:, 2 * h :],
        gains[6],
        unpack_in(sum_one[:, :h], count),
        unpack_out(sum_one[:, h : 2 * h], w),
        gains[7],
    )


def solution(mesh):
    both = ("items", "seq")
    lead = P("items", "seq", None)
    group = P("items", None)
    flat = P(both)
    tall = P(both, None)
    side = P(None, both)
    return jax.shard_map(
        body,
        mesh=mesh,
        in_specs=(
            lead, group, group,
            flat, tall, tall, flat, tall, tall, tall, tall, flat, flat, tall,
            flat, tall, side, flat, tall, flat, tall, tall, flat,
            lead,
        ),
        out_specs=(
            lead, lead,
            flat, tall, tall, flat, tall, tall, tall, tall, flat, flat, tall,
            flat, tall, side, flat, tall, flat, tall, tall, flat,
        ),
        check_vma=False,
    )
```

```python
import functools
import math

import jax
import jax.numpy as jnp
from jax import lax
from jax.experimental import pallas as pl
from jax.experimental.pallas import tpu as pltpu
from jax.sharding import PartitionSpec as P

HEAD_DIM = 64
TAPS = 31
BLOCK = 512
HALF = (TAPS - 1) // 2
EPSILON = 1e-05
NEAR = 3
KEYS = NEAR * BLOCK
RELS = 4 * BLOCK
LANES = 128
ROWS = 128
WINDOW = KEYS + LANES
BF = jnp.bfloat16
F32 = jnp.float32
AXES = ("items", "seq")
SMALL = 128


def dot(left, right):
    return jnp.dot(left, right, preferred_element_type=F32)


def dot_nt(left, right):
    return lax.dot_general(left, right, (((1,), (1,)), ((), ())), preferred_element_type=F32)


def dot_tn(left, right):
    return lax.dot_general(left, right, (((0,), (0,)), ((), ())), preferred_element_type=F32)


def tile_cut(group):
    near = LANES - 4 - 8 * group
    upper = lax.broadcasted_iota(jnp.int32, (8, LANES), 0) < 4
    lane = lax.broadcasted_iota(jnp.int32, (8, LANES), 1)
    return near, near - 4, upper, lane


def own_lanes(half):
    return lax.broadcasted_iota(jnp.int32, (1, LANES), 1) // HEAD_DIM == half


def twice(values, own):
    return jnp.where(own, values, pltpu.roll(values, HEAD_DIM, 1))


def slotted(values):
    row = lax.broadcasted_iota(jnp.int32, values.shape, 0)
    slot = lax.broadcasted_iota(jnp.int32, values.shape, 1) // HEAD_DIM
    place = 3 - row % 4
    return jnp.concatenate(
        [jnp.where(slot == place, values, 0.0), jnp.where(slot + 2 == place, values, 0.0)], axis=1
    ).astype(BF)


def four_rows(r_ref, r_scr, own):
    r_scr[0:RELS, :] = twice(r_ref[...].astype(F32), own)
    r_scr[RELS : RELS + 8, :] = jnp.zeros((8, LANES), F32)
    low = lax.broadcasted_iota(jnp.int32, (1, LANES), 1) < HEAD_DIM
    return jnp.concatenate(
        [
            jnp.where(low, r_scr[s : s + RELS, :], r_scr[s + 1 : s + 1 + RELS, :]).astype(BF)
            for s in (0, 2)
        ],
        axis=1,
    )


def positions_kernel(q_ref, r_ref, b_ref, out_ref, pos_scr, r_scr):
    own = own_lanes(pl.program_id(1))
    qb = (q_ref[...].astype(F32) + b_ref[...].astype(F32)) * HEAD_DIM**-0.5
    pos_scr[...] = dot_nt(slotted(twice(qb, own)), four_rows(r_ref, r_scr, own))

    def chunk(c, carry):
        first = (BLOCK // ROWS - 1 - c) * LANES
        for group in range(ROWS // 8):
            rows = pl.ds(pl.multiple_of(c * ROWS + 8 * group, 8), 8)
            near, far, upper, lane = tile_cut(group)
            stay = lane < LANES - jnp.where(upper, near, far)
            before = None
            for j in range(WINDOW // LANES):
                tile = pos_scr[rows, pl.ds(pl.multiple_of(first + j * LANES, LANES), LANES)]
                moved = jnp.where(
                    upper,
                    pltpu.roll(tile, LANES - near, 1),
                    pltpu.roll(tile, LANES - far, 1) if far else tile,
                )
                if j:
                    out_ref[0, rows, (j - 1) * LANES : j * LANES] = jnp.where(stay, before, moved)
                before = moved
        return carry

    lax.fori_loop(0, BLOCK // ROWS, chunk, 0)


def attend_kernel(
    live_ref, q_ref, k_ref, v_ref, u_ref, pos_ref, mix_ref, e_ref, inv_ref, s_scr, sum_scr, top_scr
):
    half = pl.program_id(1)
    own = own_lanes(half)
    scale = HEAD_DIM**-0.5
    q = q_ref[...].astype(F32)
    qm = jnp.where(own, q * scale, 0.0).astype(BF)
    um = jnp.broadcast_to(jnp.where(own, u_ref[...].astype(F32) * scale, 0.0), q.shape).astype(BF)
    k = k_ref[...]
    s_scr[...] = dot_nt(jnp.concatenate([qm, um], axis=1), jnp.concatenate([k, k], axis=1))
    keep = lax.broadcasted_iota(jnp.int32, (1, KEYS), 1) < live_ref[0]
    mask = jnp.where(keep, 0.0, -1000000000.0)

    def chunk(c, carry):
        for group in range(ROWS // 8):
            rows = pl.ds(pl.multiple_of(c * ROWS + 8 * group, 8), 8)
            top = None
            for j in range(KEYS // LANES):
                at = slice(j * LANES, (j + 1) * LANES)
                score = s_scr[rows, at] + mask[:, at] + pos_ref[0, rows, at]
                sum_scr[rows, at] = score
                top = score if top is None else jnp.maximum(top, score)
            top_scr[8 * group : 8 * group + 8, :] = top
        tops = jnp.max(top_scr[...], axis=1, keepdims=True)
        for pair in range(ROWS // 16):
            rows = pl.ds(pl.multiple_of(c * ROWS + 16 * pair, 16), 16)
            e_ref[0, rows, :] = jnp.exp(sum_scr[rows, :] - tops[16 * pair : 16 * pair + 16]).astype(BF)
        return carry

    lax.fori_loop(0, BLOCK // ROWS, chunk, 0)
    ones = jnp.where(own, v_ref[...].astype(F32), 1.0).astype(BF)
    both = dot(e_ref[0], ones)
    inverse = 1.0 / pltpu.roll(both, HEAD_DIM, 1)
    mixed = both * inverse

    @pl.when(half == 0)
    def _():
        mix_ref[...] = mixed.astype(BF)
        inv_ref[...] = inverse

    @pl.when(half == 1)
    def _():
        mix_ref[...] = jnp.where(own, mixed, mix_ref[...].astype(F32)).astype(BF)
        inv_ref[...] = jnp.where(own, inverse, inv_ref[...])


def pair_block(rows):
    return pl.BlockSpec((rows, LANES), lambda i, h: (0, i))


def head_block(frames):
    return pl.BlockSpec((1, frames, KEYS), lambda i, h: (2 * i + h, 0, 0))


def heads_call(kernel, name, ins, outs, scratch, flops, exps=0):
    pairs = next(a.shape[1] for a, _ in ins if a.ndim == 2) // LANES
    moved = sum(math.prod(a.shape) * a.dtype.itemsize for a, _ in ins)
    moved += sum(math.prod(shape) * jnp.dtype(dtype).itemsize for shape, dtype, _ in outs)
    return pl.pallas_call(
        kernel,
        grid=(pairs, 2),
        in_specs=[spec for _, spec in ins],
        out_specs=[spec for _, _, spec in outs],
        out_shape=[jax.ShapeDtypeStruct(shape, dtype) for shape, dtype, _ in outs],
        scratch_shapes=[pltpu.VMEM(shape, dtype) for shape, dtype in scratch],
        compiler_params=pltpu.CompilerParams(vmem_limit_bytes=48 * 1024 * 1024),
        cost_estimate=pl.CostEstimate(
            flops=8 * flops * 2 * pairs, bytes_accessed=moved, transcendentals=exps * 2 * pairs
        ),
        name=name,
    )(*[a for a, _ in ins])


def relative_scores(q, rel, b):
    frames, width = q.shape
    return heads_call(
        positions_kernel,
        "positions",
        [(q, pair_block(frames)), (rel, pair_block(RELS)), (b, pair_block(1))],
        [((width // HEAD_DIM, frames, KEYS), F32, head_block(frames))],
        [((frames, RELS), F32), ((RELS + 8, LANES), F32)],
        frames * RELS * LANES,
    )[0]


def attend(live, q, k, v, u, relative):
    frames, width = q.shape
    return heads_call(
        attend_kernel,
        "attend",
        [
            (live, pl.BlockSpec(memory_space=pltpu.SMEM)),
            (q, pair_block(frames)),
            (k, pair_block(KEYS)),
            (v, pair_block(KEYS)),
            (u, pair_block(1)),
            (relative, head_block(frames)),
        ],
        [
            ((frames, width), BF, pair_block(frames)),
            ((width // HEAD_DIM, frames, KEYS), BF, head_block(frames)),
            ((frames, width), F32, pair_block(frames)),
        ],
        [((frames, KEYS), F32), ((frames, KEYS), F32), ((ROWS, LANES), F32)],
        2 * frames * KEYS * LANES,
        frames * KEYS,
    )


def keys_back_kernel(
    q_ref, v_ref, u_ref, g_ref, mix_ref, inv_ref, e_ref, ds_ref, dk_ref, dv_ref, dp_scr
):
    frames = q_ref.shape[0]
    qu = (q_ref[...].astype(F32) + u_ref[...].astype(F32)) * HEAD_DIM**-0.5
    grad = g_ref[...].astype(F32) * inv_ref[...]
    lane = lax.broadcasted_iota(jnp.int32, (1, LANES), 1)
    minus = jnp.broadcast_to(jnp.where(lane < 2, -1.0, 0.0), (KEYS, LANES)).astype(BF)
    wide_v = jnp.concatenate([v_ref[...], minus], axis=1)
    qus, gms = [], []
    for half in range(2):
        own = own_lanes(half)
        qus.append(jnp.where(own, qu, 0.0).astype(BF))
        gm = jnp.where(own, grad, 0.0).astype(BF)
        total = jnp.sum(gm.astype(F32) * mix_ref[...].astype(F32), axis=1, keepdims=True)
        high = total.astype(BF).astype(F32)
        totals = jnp.where(lane == 0, high, jnp.where(lane == 1, total - high, 0.0)).astype(BF)
        dp_scr[half] = dot_nt(jnp.concatenate([gm, totals], axis=1), wide_v)
        gms.append(gm)
    gm = jnp.concatenate(gms, axis=0)
    both = e_ref[...].reshape(2 * frames, KEYS)
    dv_ref[...] = dot_tn(gm, both).T.astype(BF)

    def chunk(c, carry):
        rows = pl.ds(pl.multiple_of(c * ROWS, ROWS), ROWS)
        for half in range(2):
            for j in range(KEYS // LANES):
                at = slice(j * LANES, (j + 1) * LANES)
                ds_ref[half, rows, at] = (
                    e_ref[half, rows, at].astype(F32) * dp_scr[half, rows, at]
                ).astype(BF)
        return carry

    lax.fori_loop(0, frames // ROWS, chunk, 0)
    dk_t = dot_tn(jnp.concatenate(qus, axis=0), ds_ref[...].reshape(2 * frames, KEYS))
    dk_ref[...] = dk_t.T.astype(BF)


def pairs_call(kernel, name, ins, outs, scratch, flops):
    pairs = ins[0][0].shape[1] // LANES

    def spec(shape, rows):
        if rows:
            return pl.BlockSpec((rows, LANES), lambda i: (0, i))
        return pl.BlockSpec((2, *shape[1:]), lambda i: (i, 0, 0))

    moved = sum(math.prod(a.shape) * a.dtype.itemsize for a, _ in ins)
    moved += sum(math.prod(shape) * jnp.dtype(dtype).itemsize for shape, dtype, _ in outs)
    return pl.pallas_call(
        kernel,
        grid=(pairs,),
        in_specs=[spec(a.shape, rows) for a, rows in ins],
        out_specs=[spec(shape, rows) for shape, _, rows in outs],
        out_shape=[jax.ShapeDtypeStruct(shape, dtype) for shape, dtype, _ in outs],
        scratch_shapes=[pltpu.VMEM(shape, dtype) for shape, dtype in scratch],
        compiler_params=pltpu.CompilerParams(vmem_limit_bytes=56 * 1024 * 1024),
        cost_estimate=pl.CostEstimate(
            flops=16 * flops * pairs, bytes_accessed=moved, transcendentals=0
        ),
        name=name,
    )(*[a for a, _ in ins])


def keys_back(q, v, u, grad, mixed, inverse, weights):
    frames, width = q.shape
    return pairs_call(
        keys_back_kernel,
        "keys_back",
        [
            (q, frames),
            (v, KEYS),
            (u, 1),
            (grad, frames),
            (mixed, frames),
            (inverse, frames),
            (weights, 0),
        ],
        [
            ((width // HEAD_DIM, frames, KEYS), BF, 0),
            ((KEYS, width), BF, KEYS),
            ((KEYS, width), BF, KEYS),
        ],
        [((2, frames, KEYS), F32)],
        3 * frames * KEYS * LANES,
    )


def unskew(ds_ref, dun_scr, half, c):
    first = (BLOCK // ROWS - 1 - c) * LANES
    for pair in range(ROWS // 16):
        rows = pl.ds(pl.multiple_of(c * ROWS + 16 * pair, 16), 16)
        before = [jnp.zeros((8, LANES), F32)] * 2
        for j in range(WINDOW // LANES):
            outs = []
            if j < KEYS // LANES:
                scores = ds_ref[half, rows, j * LANES : (j + 1) * LANES].astype(F32)
            for part in range(2):
                near, far, upper, lane = tile_cut(2 * pair + part)
                if j < KEYS // LANES:
                    score = scores[8 * part : 8 * part + 8]
                    moved = jnp.where(
                        upper,
                        pltpu.roll(score, near, 1),
                        pltpu.roll(score, far, 1) if far else score,
                    )
                else:
                    moved = jnp.zeros((8, LANES), F32)
                outs.append(jnp.where(lane >= jnp.where(upper, near, far), moved, before[part]))
                before[part] = moved
            there = pl.ds(pl.multiple_of(first + j * LANES, LANES), LANES)
            dun_scr[rows, there] = jnp.concatenate(outs, axis=0).astype(BF)


def queries_back_kernel(
    q_ref, k_ref, r_ref, b_ref, ds_ref, dq_ref, dr_ref, du_ref, db_ref,
    dun0_scr, dun1_scr, r_scr, rc_scr, dqk_scr, wide_scr, four_scr,
):
    scale = HEAD_DIM**-0.5
    frames = q_ref.shape[0]
    duns = (dun0_scr, dun1_scr)
    part = RELS // (BLOCK // ROWS)

    @pl.when(pl.program_id(0) == 0)
    def _():
        dun0_scr[...] = jnp.zeros_like(dun0_scr)
        dun1_scr[...] = jnp.zeros_like(dun1_scr)

    qb = (q_ref[...].astype(F32) + b_ref[...].astype(F32)) * scale
    qbs = [slotted(twice(qb, own_lanes(half))) for half in range(2)]
    rc_scr[...] = four_rows(r_ref, r_scr, own_lanes(0))
    k = k_ref[...]

    def relative_products(half, c):
        rows = pl.ds(pl.multiple_of(c * ROWS, ROWS), ROWS)
        wide_scr[rows, :] = dot(duns[half][rows, :], rc_scr[...])
        lanes = pl.ds(pl.multiple_of(c * part, part), part)
        four_scr[:, lanes] = dot_tn(qbs[half], duns[half][:, lanes])

    def first_head(c, carry):
        rows = pl.ds(pl.multiple_of(c * ROWS, ROWS), ROWS)
        unskew(ds_ref, dun0_scr, 0, c)
        for half in range(2):
            dqk_scr[half, rows, :] = dot(ds_ref[half, rows, :], k)
        return carry

    def second_head(c, carry):
        unskew(ds_ref, dun1_scr, 1, c)
        relative_products(0, c)
        return carry

    def finish(half):
        own = own_lanes(half)
        wide = wide_scr[...] * scale
        slot = lax.broadcasted_iota(jnp.int32, (frames, LANES), 1) // HEAD_DIM
        place = 3 - lax.broadcasted_iota(jnp.int32, (frames, LANES), 0) % 4
        picked = jnp.where(slot == place, wide[:, :LANES], 0.0)
        picked += jnp.where(slot + 2 == place, wide[:, LANES:], 0.0)
        dq_r = jnp.where(own, picked + pltpu.roll(picked, HEAD_DIM, 1), 0.0)
        dq_k = jnp.where(own, dqk_scr[half] * scale, 0.0)
        four = four_scr[...]
        dr_t = four[:HEAD_DIM]
        for s in (1, 2, 3):
            dr_t += pltpu.roll(four[s * HEAD_DIM : (s + 1) * HEAD_DIM], s, 1)
        return dq_k, dq_r, dr_t

    lax.fori_loop(0, frames // ROWS, first_head, 0)
    lax.fori_loop(0, frames // ROWS, second_head, 0)
    dq_k0, dq_r0, dr_t0 = finish(0)
    rc_scr[...] = four_rows(r_ref, r_scr, own_lanes(1))
    wide_scr[...] = dot(dun1_scr[...], rc_scr[...])
    four_scr[...] = dot_tn(qbs[1], dun1_scr[...])
    dq_k1, dq_r1, dr_t1 = finish(1)
    dq_k, dq_r = dq_k0 + dq_k1, dq_r0 + dq_r1
    dq_ref[...] = (dq_k + dq_r).astype(BF)
    du_ref[...] = jnp.sum(dq_k, axis=0, keepdims=True)
    db_ref[...] = jnp.sum(dq_r, axis=0, keepdims=True)
    dr_ref[...] = jnp.concatenate([dr_t0, dr_t1], axis=0).T.astype(BF)


def queries_back(q, k, rel, b, scores):
    frames, width = q.shape
    return pairs_call(
        queries_back_kernel,
        "queries_back",
        [(q, frames), (k, KEYS), (rel, RELS), (b, 1), (scores, 0)],
        [
            ((frames, width), BF, frames),
            ((RELS, width), BF, RELS),
            ((1, width), F32, 1),
            ((1, width), F32, 1),
        ],
        [
            ((frames, RELS), BF),
            ((frames, RELS), BF),
            ((RELS + 8, LANES), F32),
            ((RELS, 2 * LANES), BF),
            ((2, frames, LANES), F32),
            ((frames, 2 * LANES), F32),
            ((2 * LANES, RELS), F32),
        ],
        frames * LANES * (KEYS + 2 * RELS),
    )


MESH = pl.DeviceIdType.MESH


def grid_of(items, seq):
    side = math.isqrt(items)
    return side, seq // 2


def whereabouts(side):
    item, place = lax.axis_index("items"), lax.axis_index("seq")
    return item // side, item % side, place // 2, place % 2


def at_device(side, y, x, z, core):
    return (y * side + x, z * 2 + core)


def meet(partners):
    barrier = pltpu.get_barrier_semaphore()
    for partner in partners:
        pl.semaphore_signal(barrier, inc=1, device_id=partner, device_id_type=MESH)
    pl.semaphore_wait(barrier, len(partners))


def all_partners(side, depth, y, x, z, core):
    return (
        [at_device(side, y, x, z, 1 - core)]
        + [at_device(side, y, (x + d) % side, z, core) for d in range(1, side)]
        + [at_device(side, (y + d) % side, x, z, core) for d in range(1, side)]
        + [at_device(side, y, x, (z + d) % depth, core) for d in range(1, depth)]
    )


def send(source, target, send_sem, recv_sem, device):
    copy = pltpu.make_async_remote_copy(
        src_ref=source, dst_ref=target, send_sem=send_sem, recv_sem=recv_sem,
        device_id=device, device_id_type=MESH,
    )
    copy.start()
    return copy


AHEAD = 6
LAG = 3


def gather_order(p):
    if p % 8 == 4:
        return "yxz" if p % 16 == 4 else "xyz"
    return "zxy" if p % 2 else "zyx"


def gather_kernel(side, depth, pieces, count, *refs):
    shards, outs = refs[:count], refs[count : 2 * count]
    own_sem, s_sem, r_sem, cs_sem, cr_sem = refs[2 * count :]
    y, x, z, core = whereabouts(side)
    meet(all_partners(side, depth, y, x, z, core))
    owns = [
        pltpu.make_async_copy(shard, out.at[y, x, z, core], own_sem.at[i])
        for i, (shard, out) in enumerate(zip(shards, outs))
    ]
    for own in owns:
        own.start()
    copies = {}

    def region(p, done):
        i, cols = pieces[p]
        every = slice(None)
        return outs[i].at[
            every if "y" in done else y,
            every if "x" in done else x,
            every if "z" in done else z,
            core, :, cols,
        ]

    def start(p, k):
        order = gather_order(p)
        axis = order[k]
        here = region(p, order[:k])
        i, cols = pieces[p]
        copies[p, k] = [
            send(
                here if k else shards[i].at[:, cols], here,
                s_sem.at[k, p, d - 1], r_sem.at[k, p, d - 1],
                at_device(
                    side,
                    (y + d) % side if axis == "y" else y,
                    (x + d) % side if axis == "x" else x,
                    (z + d) % depth if axis == "z" else z,
                    core,
                ),
            )
            for d in range(1, depth if axis == "z" else side)
        ]

    def arrived(p, k):
        for copy in copies[p, k]:
            copy.wait_recv()

    for p in range(min(AHEAD, len(pieces))):
        start(p, 0)
    for own in owns:
        own.wait()
    for t in range(len(pieces) + 3 * LAG):
        if t + AHEAD < len(pieces):
            start(t + AHEAD, 0)
        for k in (1, 2):
            p = t - (k - 1) * LAG
            if 0 <= p < len(pieces):
                arrived(p, k - 1)
                start(p, k)
        p = t - 2 * LAG
        if 0 <= p < len(pieces):
            arrived(p, 2)
            here = region(p, "yxz")
            copies[p, 3] = [
                send(here, here, cs_sem.at[p], cr_sem.at[p], at_device(side, y, x, z, 1 - core))
            ]
        p = t - 3 * LAG
        if 0 <= p < len(pieces):
            arrived(p, 3)
    for started in copies.values():
        for copy in started:
            copy.wait_send()


def gather_by_kernel(shards, side, depth):
    pieces = [
        (i, pl.ds(c, min(512, shard.shape[1])))
        for i, shard in enumerate(shards)
        for c in range(0, shard.shape[1], 512)
    ]
    dma = pltpu.SemaphoreType.DMA
    n = len(pieces)
    outs = pl.pallas_call(
        functools.partial(gather_kernel, side, depth, pieces, len(shards)),
        in_specs=[pl.BlockSpec(memory_space=pl.ANY)] * len(shards),
        out_specs=[pl.BlockSpec(memory_space=pl.ANY)] * len(shards),
        out_shape=[
            jax.ShapeDtypeStruct((side, side, depth, 2, *shard.shape), shard.dtype)
            for shard in shards
        ],
        scratch_shapes=[dma((len(shards),))]
        + [dma((3, n, max(side, depth) - 1))] * 2
        + [dma((n,))] * 2,
        compiler_params=pltpu.CompilerParams(
            collective_id=1, has_side_effects=True, vmem_limit_bytes=48 * 1024 * 1024
        ),
        name="gather",
    )(*shards)
    return [out.reshape(-1, out.shape[-1]) for out in outs]


def put_block(out_ref, piece, total):
    rows = total.shape[0]
    lane = lax.broadcasted_iota(jnp.int32, (rows, LANES), 1)
    each = LANES // 4
    for tile in range(total.shape[1] // LANES):
        some = total[:, tile * LANES : (tile + 1) * LANES]
        for q in range(4):
            turn = (each * (piece - q)) % LANES
            moved = pltpu.roll(some, turn, 1) if turn else some
            at = slice((4 * tile + q) * LANES, (4 * tile + q + 1) * LANES)
            rest = out_ref[:, at] if piece else jnp.zeros_like(some)
            out_ref[:, at] = jnp.where(lane // each == piece, moved, rest)


Z_FIRST = (6, 12)


def added(parts):
    if len(parts) == 2:
        return parts[0] + parts[1]
    return sum(part.astype(F32) for part in parts).astype(BF)


def scatter_kernel(side, depth, pieces, count, *refs):
    ops, (small_out, four_out, in_out, out_out) = refs[:count], refs[count : count + 4]
    l_buf, r_buf, sum_buf, g_buf, c_buf, a_buf, b_buf, z_buf = refs[count + 4 : count + 12]
    e_buf, f_buf, h_buf = refs[count + 12 : count + 15]
    l_sem, r_sem, cs_sem, cr_sem, as_sem, ar_sem, bs_sem, br_sem, zs_sem, zr_sem = refs[count + 15 :]
    y, x, z, core = whereabouts(side)
    rows, wide = g_buf.shape[-2:]
    section = depth * 2 * rows
    last = len(pieces)
    meet(all_partners(side, depth, y, x, z, core))

    def cols(p):
        return pl.ds(0, pieces[p][5])

    def z_first(p):
        return Z_FIRST.index(p) if p in Z_FIRST else None

    most = l_buf.shape[1]
    chunks = []
    for p, (left, *_) in enumerate(pieces):
        deep = most if left is None else ops[left].shape[0]
        chunks += [(p, k, min(most, deep - k)) for k in range(0, deep, most)]

    def load(s):
        p, k, many = chunks[s]
        left, left_at, right, right_at, place, many_cols = pieces[p]
        slot = s % 2
        if left is None:
            copies = [
                pltpu.make_async_copy(
                    ops[right], g_buf.at[p % 2, :, :, :, :, :, cols(p)], r_sem.at[slot]
                )
            ]
        else:
            copies = [
                pltpu.make_async_copy(
                    ops[left].at[pl.ds(k, many), pl.ds(left_at, wide)],
                    l_buf.at[slot, pl.ds(0, many)], l_sem.at[slot],
                ),
                pltpu.make_async_copy(
                    ops[right].at[pl.ds(k, many), pl.ds(right_at, many_cols)],
                    r_buf.at[slot, pl.ds(0, many), cols(p)], r_sem.at[slot],
                ),
            ]
        for copy in copies:
            copy.start()
        return copies

    def multiply(s):
        p, k, many = chunks[s]
        slot = s % 2
        first, final = k == 0, k + many == ops[pieces[p][0]].shape[0]

        def section_product(i, carry):
            lanes = pl.ds(pl.multiple_of(i * section, section), section)
            total = dot_tn(l_buf[slot, 0:many, lanes], r_buf[slot, 0:many, cols(p)])
            if not first:
                total += sum_buf[lanes, cols(p)]
            if final:
                total = total.astype(BF).reshape(depth, 2, rows, pieces[p][5])
                g_buf[p % 2, i // side, i % side, :, :, :, cols(p)] = total
            else:
                sum_buf[lanes, cols(p)] = total
            return carry

        lax.fori_loop(0, side * side, section_product, 0)

    c_copies, a_copies, b_copies, z_copies = [], [], [], []
    loads = [load(0)]
    for t in range(last + 1 + 3 * LAG):
        p = t
        if p < last:
            if p >= 2:
                c_copies[p - 2].wait_send()
            for s in [s for s in range(len(chunks)) if chunks[s][0] == p]:
                if s + 1 < len(chunks):
                    loads.append(load(s + 1))
                for copy in loads[s]:
                    copy.wait()
                if pieces[p][0] is not None:
                    multiply(s)
            c_copies.append(
                send(
                    g_buf.at[p % 2, :, :, :, 1 - core, :, cols(p)],
                    c_buf.at[p, :, :, :, :, cols(p)],
                    cs_sem.at[p], cr_sem.at[p], at_device(side, y, x, z, 1 - core),
                )
            )
        p = t - 1
        if 0 <= p < last:
            c_copies[p].wait_recv()

            def add_core(i, carry, p=p):
                at = (i // side, i % side)
                c_buf[p, *at, :, :, cols(p)] += g_buf[p % 2, *at, :, core, :, cols(p)]
                return carry

            lax.fori_loop(0, side * side, add_core, 0)
            a_copies.append(
                [
                    send(
                        c_buf.at[p, :, :, (z + d) % depth, :, cols(p)],
                        e_buf.at[z_first(p), d - 1, :, :, :, cols(p)],
                        as_sem.at[p, d - 1], ar_sem.at[p, d - 1],
                        at_device(side, y, x, (z + d) % depth, core),
                    )
                    for d in range(1, depth)
                ]
                if z_first(p) is not None
                else [
                    send(
                        c_buf.at[p, (y + d) % side, :, :, :, cols(p)]
                        if p % 2
                        else c_buf.at[p, :, (x + d) % side, :, :, cols(p)],
                        a_buf.at[p, d - 1, :, :, :, cols(p)],
                        as_sem.at[p, d - 1], ar_sem.at[p, d - 1],
                        at_device(side, (y + d) % side, x, z, core)
                        if p % 2
                        else at_device(side, y, (x + d) % side, z, core),
                    )
                    for d in range(1, side)
                ]
            )
        p = t - 1 - LAG
        if 0 <= p < last:
            for copy in a_copies[p]:
                copy.wait_recv()

            def add_first(j, carry, p=p):
                own = c_buf[p, y, j, :, :, cols(p)] if p % 2 else c_buf[p, j, x, :, :, cols(p)]
                a_buf[p, 0, j, :, :, cols(p)] = added(
                    [own] + [a_buf[p, d, j, :, :, cols(p)] for d in range(side - 1)]
                )
                return carry

            q = z_first(p)
            if q is None:
                lax.fori_loop(0, side, add_first, 0)
            else:
                for j in range(side):
                    e_buf[q, 0, j, :, :, cols(p)] = added(
                        [c_buf[p, j, :, z, :, cols(p)]]
                        + [e_buf[q, d, j, :, :, cols(p)] for d in range(depth - 1)]
                    )
            b_copies.append(
                [
                    send(
                        e_buf.at[q, 0, :, (x + d) % side, :, cols(p)],
                        f_buf.at[q, d - 1, :, :, cols(p)],
                        bs_sem.at[p, d - 1], br_sem.at[p, d - 1],
                        at_device(side, y, (x + d) % side, z, core),
                    )
                    for d in range(1, side)
                ]
                if q is not None
                else [
                    send(
                        a_buf.at[p, 0, ((x if p % 2 else y) + d) % side, :, :, cols(p)],
                        b_buf.at[p, d - 1, :, :, cols(p)],
                        bs_sem.at[p, d - 1], br_sem.at[p, d - 1],
                        at_device(side, y, (x + d) % side, z, core)
                        if p % 2
                        else at_device(side, (y + d) % side, x, z, core),
                    )
                    for d in range(1, side)
                ]
            )
        p = t - 1 - 2 * LAG
        if 0 <= p < last:
            for copy in b_copies[p]:
                copy.wait_recv()

            q = z_first(p)
            if q is None:
                own = a_buf[p, 0, x if p % 2 else y, :, :, cols(p)]
                b_buf[p, 0, :, :, cols(p)] = added(
                    [own] + [b_buf[p, d, :, :, cols(p)] for d in range(side - 1)]
                )
            else:
                f_buf[q, 0, :, :, cols(p)] = added(
                    [e_buf[q, 0, :, x, :, cols(p)]]
                    + [f_buf[q, d, :, :, cols(p)] for d in range(side - 1)]
                )
            z_copies.append(
                [
                    send(
                        f_buf.at[q, 0, (y + d) % side, :, cols(p)],
                        h_buf.at[q, d - 1, :, cols(p)],
                        zs_sem.at[p, d - 1], zr_sem.at[p, d - 1],
                        at_device(side, (y + d) % side, x, z, core),
                    )
                    for d in range(1, side)
                ]
                if q is not None
                else [
                    send(
                        b_buf.at[p, 0, (z + d) % depth, :, cols(p)],
                        z_buf.at[p, d - 1, :, cols(p)],
                        zs_sem.at[p, d - 1], zr_sem.at[p, d - 1],
                        at_device(side, y, x, (z + d) % depth, core),
                    )
                    for d in range(1, depth)
                ]
            )
        p = t - 1 - 3 * LAG
        if 0 <= p < last:
            for copy in z_copies[p]:
                copy.wait_recv()
            q = z_first(p)
            total = (b_buf[p, 0, z, :, cols(p)] if q is None else f_buf[q, 0, y, :, cols(p)]).astype(F32)
            for d in range(depth - 1 if q is None else side - 1):
                total += (z_buf[p, d, :, cols(p)] if q is None else h_buf[q, d, :, cols(p)]).astype(F32)
            kind, index = pieces[p][4]
            if kind == 0:
                small_out[...] = total
            elif kind == 1:
                four_out[index] = total
            elif kind == 2:
                put_block(in_out, index, total)
            else:
                at = pieces[p][3]
                out_out[index * rows : (index + 1) * rows, at : at + pieces[p][5]] = total
    for p in range(last):
        for copy in ([c_copies[p]] if p >= last - 2 else []) + a_copies[p] + b_copies[p] + z_copies[p]:
            copy.wait_send()


def scatter_by_kernel(pairs, before, active, hidden, low, small, side, depth):
    width = low.shape[1]
    rows = width // (side * side * depth * 2)
    ops, pieces = [], []

    def operand(array):
        ops.append(array)
        return len(ops) - 1

    slabs = small.reshape(side, side, depth, 2, rows, small.shape[1])
    pieces.append((None, 0, operand(slabs), 0, (0, 0), small.shape[1]))
    seen, many = {}, 0
    for left, right in pairs:
        if id(left) not in seen:
            seen[id(left)] = operand(left)
        at_right = operand(right)
        for c in range(0, right.shape[1], width):
            pieces.append((seen[id(left)], 0, at_right, c, (1, many), width))
            many += 1
    at_hidden, at_before = operand(hidden), operand(before)
    at_active, at_low = operand(active), operand(low)
    steps = range(before.shape[1] // width)
    pieces += [(at_hidden, 0, at_before, c * width, (2, c), width) for c in steps]
    pieces += [(at_active, c * width, at_low, 0, (3, c), width) for c in steps]
    last = pieces.pop()
    pieces += [(*last[:3], at, last[4], width // 2) for at in (0, width // 2)]
    n = len(pieces)
    dma = pltpu.SemaphoreType.DMA
    outs = (
        (rows, small.shape[1]),
        (many, rows, width),
        (rows, before.shape[1]),
        (rows * len(steps), width),
    )
    return pl.pallas_call(
        functools.partial(scatter_kernel, side, depth, pieces, len(ops)),
        in_specs=[pl.BlockSpec(memory_space=pl.ANY)] * len(ops),
        out_specs=[pl.BlockSpec(memory_space=pltpu.VMEM)] * len(outs),
        out_shape=[jax.ShapeDtypeStruct(shape, F32) for shape in outs],
        scratch_shapes=[
            pltpu.VMEM((2, width, width), BF),
            pltpu.VMEM((2, width, width), BF),
            pltpu.VMEM((width, width), F32),
            pltpu.VMEM((2, side, side, depth, 2, rows, width), BF),
            pltpu.VMEM((n, side, side, depth, rows, width), BF),
            pltpu.VMEM((n, side - 1, side, depth, rows, width), BF),
            pltpu.VMEM((n, side - 1, depth, rows, width), BF),
            pltpu.VMEM((n, depth - 1, rows, width), BF),
            pltpu.VMEM((len(Z_FIRST), depth - 1, side, side, rows, width), BF),
            pltpu.VMEM((len(Z_FIRST), side - 1, side, rows, width), BF),
            pltpu.VMEM((len(Z_FIRST), side - 1, rows, width), BF),
            dma((2,)),
            dma((2,)),
            dma((n,)),
            dma((n,)),
        ]
        + [dma((n, max(side, depth) - 1))] * 6,
        compiler_params=pltpu.CompilerParams(
            collective_id=2, has_side_effects=True, vmem_limit_bytes=58 * 1024 * 1024
        ),
        name="scatter",
    )(*ops)


def products_kernel(ranges, *refs):
    p = pl.program_id(0)
    out_ref = refs[-1]
    section = 512
    for i, (first, count) in enumerate(ranges):
        left_ref, right_ref = refs[2 * i], refs[2 * i + 1]

        @pl.when((p >= first) & (p < first + count))
        def _(left_ref=left_ref, right_ref=right_ref):
            def part(j, carry):
                some = pl.ds(pl.multiple_of(j * section, section), section)
                out_ref[some, :] = dot_tn(left_ref[:, some], right_ref[...]).astype(BF)
                return carry

            lax.fori_loop(0, out_ref.shape[0] // section, part, 0)


def products(pairs):
    frames, width = pairs[0][0].shape
    specs, ops, ranges, first = [], [], [], 0
    for left, right in pairs:
        count = max(left.shape[1], right.shape[1]) // width
        for array in (left, right):
            most = array.shape[1] // width - 1
            specs.append(
                pl.BlockSpec(
                    (frames, width), lambda p, first=first, most=most: (0, jnp.clip(p - first, 0, most))
                )
            )
            ops.append(array)
        ranges.append((first, count))
        first += count
    return pl.pallas_call(
        functools.partial(products_kernel, ranges),
        grid=(first,),
        in_specs=specs,
        out_specs=pl.BlockSpec((width, width), lambda p: (0, p)),
        out_shape=jax.ShapeDtypeStruct((width, first * width), BF),
        compiler_params=pltpu.CompilerParams(vmem_limit_bytes=48 * 1024 * 1024),
        cost_estimate=pl.CostEstimate(
            flops=2 * frames * width * width * first,
            bytes_accessed=(3 * frames + 2 * width) * width * first,
            transcendentals=0,
        ),
        name="products",
    )(*ops)


def by_kernel(rows):
    items, seq = lax.axis_size("items"), lax.axis_size("seq")
    return rows % 16 == 0 and math.isqrt(items) ** 2 == items and items > 1 and seq > 2 and seq % 2 == 0


def norm(values):
    center = values - jnp.mean(values, axis=-1, keepdims=True)
    spread = jnp.mean(center * center, axis=-1, keepdims=True)
    scale = lax.rsqrt(spread + EPSILON)
    return center * scale, scale


def norm_back(grad, unit, scale, gain):
    inner = grad * gain
    mean_inner = jnp.mean(inner, axis=-1, keepdims=True)
    mean_both = jnp.mean(inner * unit, axis=-1, keepdims=True)
    return scale * (inner - mean_inner - unit * mean_both), jnp.sum(grad * unit, axis=0)


def silu_slope(value):
    s = jax.nn.sigmoid(value)
    return s * (1.0 + value * (1.0 - s))


def pack_in(shard, count):
    rows, hidden = shard.shape
    pieces = hidden // count // rows
    if 4 * rows == LANES and pieces == 4:
        return reorder(shard, True, shard.dtype)
    return shard.reshape(rows, count, pieces, rows).transpose(0, 2, 1, 3).reshape(rows, hidden)


def unpack_in(shard, count):
    rows, hidden = shard.shape
    pieces = hidden // count // rows
    if 4 * rows == LANES and pieces == 4:
        return reorder(shard, False, F32)
    return shard.reshape(rows, pieces, count, rows).transpose(0, 2, 1, 3).reshape(rows, hidden)


def pack_out(shard, rows):
    pieces, width = shard.shape[0] // rows, shard.shape[1]
    return shard.reshape(pieces, rows, width).transpose(1, 0, 2).reshape(rows, pieces * width)


def unpack_out(shard, width):
    rows, pieces = shard.shape[0], shard.shape[1] // width
    return shard.reshape(rows, pieces, width).transpose(1, 0, 2).reshape(rows * pieces, width)


def reorder_kernel(to_pieces, in_ref, out_ref):
    each = LANES // 4
    tiles = in_ref.shape[1] // LANES // 4
    lane = lax.broadcasted_iota(jnp.int32, (in_ref.shape[0], LANES), 1)

    def tile(at):
        return in_ref[:, at * LANES : (at + 1) * LANES].astype(F32)

    for k in range(tiles):
        for c in range(4):
            total = None
            for q in range(4):
                some = tile(4 * k + q) if to_pieces else tile(q * tiles + k)
                turn = each * (q - c) % LANES
                some = pltpu.roll(some, turn, 1) if turn else some
                total = some if total is None else jnp.where(lane // each == q, some, total)
            at = (c * tiles + k) if to_pieces else (4 * k + c)
            out_ref[:, at * LANES : (at + 1) * LANES] = total.astype(out_ref.dtype)


def reorder(shard, to_pieces, dtype):
    return pl.pallas_call(
        functools.partial(reorder_kernel, to_pieces),
        out_shape=jax.ShapeDtypeStruct(shard.shape, dtype),
        name="reorder",
    )(shard)


def halves(size):
    return [pl.ds(0, size // 2), pl.ds(size // 2, size // 2)]


def feed_forward_kernel(hid_ref, in_ref, out_w_ref, active_ref, slope_ref, out_ref):
    @pl.when(pl.program_id(0) == 0)
    def _():
        out_ref[...] = jnp.zeros_like(out_ref)

    parts = halves(in_ref.shape[1])
    befores = [dot(hid_ref[...], in_ref[:, at]) for at in parts]
    actives = []
    for at, before in zip(parts, befores):
        gate = jax.nn.sigmoid(before)
        active = (before * gate).astype(BF)
        active_ref[:, at] = active
        slope_ref[:, at] = (gate * (1.0 + before * (1.0 - gate))).astype(BF)
        actives.append(active)
    out_ref[...] += sum(dot(active, out_w_ref[at, :]) for at, active in zip(parts, actives))


def feed_forward_back_kernel(low_ref, in_ref, out_w_ref, slope_ref, before_ref, hid_ref):
    @pl.when(pl.program_id(0) == 0)
    def _():
        hid_ref[...] = jnp.zeros_like(hid_ref)

    parts = halves(in_ref.shape[1])
    actives = [dot_nt(low_ref[...], out_w_ref[at, :]) for at in parts]
    befores = []
    for at, active in zip(parts, actives):
        before = (active * slope_ref[:, at].astype(F32)).astype(BF)
        before_ref[:, at] = before
        befores.append(before)
    hid_ref[...] += sum(dot_nt(before, in_ref[:, at]) for at, before in zip(parts, befores))


def hidden_blocks(frames, width, hidden_width):
    step = width // 2
    per = width // step
    return (
        hidden_width // step,
        pl.BlockSpec((frames, width), lambda j: (0, 0)),
        pl.BlockSpec((width, step), lambda j: (0, j)),
        pl.BlockSpec((step, width), lambda j: (j % per, j // per)),
        pl.BlockSpec((frames, step), lambda j: (0, j)),
    )


def feed_forward(hidden, weight_in, weight_out):
    frames, width = hidden.shape
    hidden_width = weight_in.shape[1]
    steps, whole, in_block, out_block, unit_block = hidden_blocks(frames, width, hidden_width)
    units = jax.ShapeDtypeStruct((frames, hidden_width), BF)
    return pl.pallas_call(
        feed_forward_kernel,
        grid=(steps,),
        in_specs=[whole, in_block, out_block],
        out_specs=[unit_block, unit_block, whole],
        out_shape=[units, units, jax.ShapeDtypeStruct((frames, width), F32)],
        compiler_params=pltpu.CompilerParams(vmem_limit_bytes=48 * 1024 * 1024),
        cost_estimate=pl.CostEstimate(
            flops=4 * frames * width * hidden_width,
            bytes_accessed=4 * (width + frames) * hidden_width,
            transcendentals=frames * hidden_width,
        ),
        name="feed_forward",
    )(hidden, weight_in, weight_out)


def feed_forward_back(grad, slope, weight_in, weight_out):
    frames, width = grad.shape
    hidden_width = weight_in.shape[1]
    low = (0.5 * grad).astype(BF)
    steps, whole, in_block, out_block, unit_block = hidden_blocks(frames, width, hidden_width)
    before, hid = pl.pallas_call(
        feed_forward_back_kernel,
        grid=(steps,),
        in_specs=[whole, in_block, out_block, unit_block],
        out_specs=[unit_block, whole],
        out_shape=[
            jax.ShapeDtypeStruct((frames, hidden_width), BF),
            jax.ShapeDtypeStruct((frames, width), F32),
        ],
        compiler_params=pltpu.CompilerParams(vmem_limit_bytes=48 * 1024 * 1024),
        cost_estimate=pl.CostEstimate(
            flops=4 * frames * width * hidden_width,
            bytes_accessed=4 * (width + frames) * hidden_width,
            transcendentals=0,
        ),
        name="feed_forward_back",
    )(low, weight_in, weight_out, slope)
    return hid, before, low


def depthwise_kernel(wide_ref, taps_ref, out_ref):
    step = 64
    for first in range(0, out_ref.shape[0], step):
        total = jnp.zeros((step, LANES), F32)
        for k in range(TAPS):
            total += taps_ref[k : k + 1, :] * wide_ref[first + k : first + k + step, :]
        out_ref[first : first + step, :] = total


def depthwise(wide, taps):
    rows, width = wide.shape
    column = lambda rows: pl.BlockSpec((rows, LANES), lambda i: (0, i))
    return pl.pallas_call(
        depthwise_kernel,
        grid=(width // LANES,),
        in_specs=[column(rows), column(TAPS)],
        out_specs=column(rows - 2 * HALF),
        out_shape=jax.ShapeDtypeStruct((rows - 2 * HALF, width), F32),
        cost_estimate=pl.CostEstimate(
            flops=2 * rows * width * TAPS, bytes_accessed=8 * rows * width, transcendentals=0
        ),
        name="depthwise",
    )(wide, taps)


def depthwise_back_kernel(wide_ref, grad_ref, taps_ref, out_ref, dtaps_ref):
    step = 64
    frames = out_ref.shape[0]
    for first in range(0, frames, step):
        total = jnp.zeros((step, LANES), F32)
        for k in range(TAPS):
            at = first + 2 * HALF - k
            total += taps_ref[k : k + 1, :] * grad_ref[at : at + step, :]
        out_ref[first : first + step, :] = total
    sums = [jnp.zeros((8, LANES), F32)] * TAPS
    for first in range(0, frames, 8):
        grad = grad_ref[first + HALF : first + HALF + 8, :]
        sums = [sums[k] + grad * wide_ref[first + k : first + k + 8, :] for k in range(TAPS)]
    for k in range(TAPS):
        dtaps_ref[k : k + 1, :] = jnp.sum(sums[k], axis=0, keepdims=True)


def depthwise_back(wide, grad, taps):
    rows, width = wide.shape
    frames = rows - 2 * HALF
    column = lambda rows: pl.BlockSpec((rows, LANES), lambda i: (0, i))
    return pl.pallas_call(
        depthwise_back_kernel,
        grid=(width // LANES,),
        in_specs=[column(rows), column(rows), column(TAPS)],
        out_specs=[column(frames), column(TAPS)],
        out_shape=[
            jax.ShapeDtypeStruct((frames, width), F32),
            jax.ShapeDtypeStruct((TAPS, width), F32),
        ],
        cost_estimate=pl.CostEstimate(
            flops=4 * rows * width * TAPS, bytes_accessed=12 * rows * width, transcendentals=0
        ),
        name="depthwise_back",
    )(wide, grad, taps)


def shifted(values, by):
    size = lax.axis_size("seq")
    pairs = [(i, i + by) for i in range(size) if 0 <= i + by < size]
    return lax.ppermute(values, "seq", pairs)


def all_gather(shard):
    return lax.all_gather(shard, AXES, axis=0, tiled=True)


def gather_each(shards):
    if by_kernel(shards[0].shape[0]):
        side, depth = grid_of(lax.axis_size("items"), lax.axis_size("seq"))
        return gather_by_kernel(shards, side, depth)
    return [all_gather(shard) for shard in shards]


def scatter_sum(grads):
    return lax.psum_scatter(grads, AXES, scatter_dimension=0, tiled=True)


def scatter_each(pairs, before, active, hidden, low, small):
    count = lax.axis_size("items") * lax.axis_size("seq")
    width = low.shape[1]
    rows = width // count
    if by_kernel(rows):
        side, depth = grid_of(lax.axis_size("items"), lax.axis_size("seq"))
        return scatter_by_kernel(pairs, before, active, hidden, low, small, side, depth)
    steps = range(0, before.shape[1], width)
    columns = [small] + [dot_tn(left, right).astype(BF) for left, right in pairs]
    many = sum(right.shape[1] for left, right in pairs)
    columns.append(dot_tn(hidden, before).astype(BF))
    columns += [dot_tn(active[:, c : c + width], low).astype(BF) for c in steps]
    total = scatter_sum(jnp.concatenate(columns, axis=1)).astype(F32)
    small, total = total[:, : small.shape[1]], total[:, small.shape[1] :]
    return (
        small,
        [total[:, i : i + width] for i in range(0, many, width)],
        unpack_in(total[:, many : many + before.shape[1]], count),
        unpack_out(total[:, many + before.shape[1] :], width),
    )


def after(value, earlier):
    return value + jnp.minimum(jnp.abs(earlier[0, 0]), 0).astype(value.dtype)


def body(
    features, item_spans, item_lengths,
    ffn1_gain, ffn1_in, ffn1_out, att_gain, w_query, w_key, w_value, w_pos, u_bias, v_bias, w_out,
    conv_gain, conv_in, depth_kernel, inner_gain, conv_out, ffn2_gain, ffn2_in, ffn2_out, final_gain,
    cotangent,
):
    count = lax.axis_size("items") * lax.axis_size("seq")
    block = lax.axis_index("seq")
    frames, width = features.shape[1], features.shape[2]
    rows = w_query.shape[0]
    hidden_width = ffn1_in.shape[1]

    spans, lengths = item_spans[0], item_lengths[0]
    places = jnp.arange(spans.shape[0], dtype=jnp.int32)
    starts = lax.cummax(jnp.where(spans > 0, places, 0), axis=0)
    start = jnp.take(starts, block)
    live = jnp.take(lengths, start)
    place = block - start
    near_before = jnp.where((block > 0) & (jnp.take(starts, jnp.maximum(block - 1, 0)) == start), 1.0, 0.0)
    last = spans.shape[0] - 1
    near_after = jnp.where((block < last) & (jnp.take(starts, jnp.minimum(block + 1, last)) == start), 1.0, 0.0)
    live_mask = (place * BLOCK + jnp.arange(frames, dtype=jnp.int32) < live).astype(F32)[:, None]

    singles = [ffn1_gain, att_gain, u_bias, v_bias, conv_gain, inner_gain, ffn2_gain, final_gain]
    order = lax.broadcasted_iota(jnp.int32, (len(singles), rows), 0)
    vectors = jnp.broadcast_to(singles[0][None], order.shape)
    for i, single in enumerate(singles):
        vectors = jnp.where(order == i, single[None], vectors)
    small = jnp.concatenate([depth_kernel, vectors], axis=0)
    small = jnp.pad(small, ((0, SMALL - small.shape[0]), (0, 0))).T
    table, w1_in, w1_out, w_q, w_k, w_v, w_r = gather_each(
        [small, pack_in(ffn1_in, count), pack_out(ffn1_out, rows), w_query, w_key, w_value, w_pos]
    )
    set_two = all_gather(
        jnp.concatenate(
            [
                after(w_out, w_r), conv_in, conv_out,
                pack_in(ffn2_in, count), pack_out(ffn2_out, rows),
            ],
            axis=1,
        )
    )
    table = table.T.astype(F32)
    taps = table[:TAPS]
    g_ffn1, g_att, g_u, g_v, g_conv, g_inner, g_ffn2, g_final = (table[TAPS + i] for i in range(8))
    w_o = set_two[:, :width]
    c_in = set_two[:, width : 3 * width]
    c_out = set_two[:, 3 * width : 4 * width]
    w2_in = set_two[:, 4 * width : 4 * width + hidden_width]
    w2_out = set_two[:, 4 * width + hidden_width :]

    distance = (BLOCK - 1 + BLOCK * place - jnp.arange(RELS, dtype=jnp.int32)).astype(F32)
    frequency = 1.0 / 10000.0 ** (jnp.arange(0, width, 2).astype(F32) / width)
    angles = distance[:, None] * frequency[None, :]
    waves = jnp.concatenate([jnp.sin(angles), jnp.cos(angles)], axis=1).astype(BF)

    stream = features[0]
    unit1, scale1 = norm(stream)
    hid1 = (unit1 * g_ffn1).astype(BF)
    active1, slope1, out1 = feed_forward(hid1, w1_in, w1_out)
    first = stream + 0.5 * out1

    unit2, scale2 = norm(first)
    hid2 = (unit2 * g_att).astype(BF)
    nearby = [shifted(hid2, 2), shifted(hid2, 1), hid2, shifted(hid2, -1), shifted(hid2, -2)]
    queries = dot(hid2, w_q).astype(BF)
    relative = dot(waves, w_r).astype(BF)
    u_row, v_row = g_u[None].astype(BF), g_v[None].astype(BF)
    positional = relative_scores(queries, relative, v_row)
    key_hid = lax.dynamic_slice_in_dim(jnp.concatenate(nearby, axis=0), (2 - place) * BLOCK, KEYS, 0)
    keys = dot(key_hid, w_k).astype(BF)
    values = dot(key_hid, w_v).astype(BF)
    mixed, shares, inverses = attend(live.reshape(1), queries, keys, values, u_row, positional)
    second = first + dot(mixed, w_o)

    unit3, scale3 = norm(second)
    hid3 = (unit3 * g_conv).astype(BF)
    doubled = dot(hid3, c_in)
    linear, gate = doubled[:, :width], jax.nn.sigmoid(doubled[:, width:])
    glu = (linear * gate * live_mask).astype(BF)
    wide = jnp.concatenate(
        [
            shifted(glu[frames - HALF :], 1).astype(F32) * near_before,
            glu.astype(F32),
            shifted(glu[:HALF], -1).astype(F32) * near_after,
        ],
        axis=0,
    )
    depth = depthwise(wide, taps)
    unit4, scale4 = norm(depth)
    inner = unit4 * g_inner
    active4 = jax.nn.silu(inner).astype(BF)
    third = second + dot(active4, c_out)

    unit5, scale5 = norm(third)
    hid5 = (unit5 * g_ffn2).astype(BF)
    active5, slope5, out5 = feed_forward(hid5, w2_in, w2_out)
    fourth = third + 0.5 * out5
    unit6, scale6 = norm(fourth)
    layer_out = unit6 * g_final

    grad, d_final = norm_back(cotangent[0], unit6, scale6, g_final)
    d_hid5, d_before5, low5 = feed_forward_back(grad, slope5, w2_in, w2_out)
    d_third, d_ffn2 = norm_back(d_hid5, unit5, scale5, g_ffn2)
    grad = grad + d_third
    low4 = grad.astype(BF)
    packed, low4 = lax.optimization_barrier(
        (products([(hid5, d_before5), (active5, low5), (active4, low4)]), low4)
    )
    sum_one = scatter_sum(packed)

    d_active4 = dot_nt(low4, c_out)
    d_depth, d_inner = norm_back(d_active4 * silu_slope(inner), unit4, scale4, g_inner)
    d_depth = d_depth.astype(BF)
    d_wide = jnp.concatenate(
        [
            shifted(d_depth[frames - HALF :], 1).astype(F32) * near_before,
            d_depth.astype(F32),
            shifted(d_depth[:HALF], -1).astype(F32) * near_after,
        ],
        axis=0,
    )
    d_glu, d_taps = depthwise_back(wide, d_wide, taps)
    d_glu = d_glu * live_mask
    d_doubled = jnp.concatenate(
        [(d_glu * gate).astype(BF), (d_glu * linear * gate * (1.0 - gate)).astype(BF)], axis=1
    )
    d_second, d_conv = norm_back(dot_nt(d_doubled, c_in), unit3, scale3, g_conv)
    grad = grad + d_second

    low2 = grad.astype(BF)
    d_mixed = dot_nt(low2, w_o).astype(BF)
    d_scores, d_k, d_v = keys_back(queries, values, u_row, d_mixed, mixed, inverses, shares)
    d_near = dot_nt(d_k, w_k) + dot_nt(d_v, w_v)
    d_own = lax.dynamic_slice_in_dim(d_near, place * BLOCK, BLOCK, 0)
    d_all = lax.dynamic_update_slice_in_dim(
        jnp.zeros((5 * BLOCK, width), BF), d_near.astype(BF), (2 - place) * BLOCK, 0
    )
    returned = [
        shifted(d_all[(2 + by) * BLOCK : (3 + by) * BLOCK], by).astype(F32) for by in (-2, -1, 1, 2)
    ]
    d_q, d_r, d_u, d_b = queries_back(queries, keys, relative, v_row, d_scores)
    d_hid2 = dot_nt(d_q, w_q) + d_own + sum(returned)
    d_first, d_att = norm_back(d_hid2, unit2, scale2, g_att)
    grad = grad + d_first

    d_hid1, d_before1, low1 = feed_forward_back(grad, slope1, w1_in, w1_out)
    d_stream, d_ffn1 = norm_back(d_hid1, unit1, scale1, g_ffn1)
    input_grad = grad + d_stream

    vectors = jnp.stack([d_ffn1, d_att, d_u[0], d_b[0], d_conv, d_inner, d_ffn2, d_final], axis=0)
    small = jnp.concatenate([d_taps, vectors], axis=0)
    small = jnp.pad(small, ((0, SMALL - small.shape[0]), (0, 0))).T.astype(BF)
    small, input_grad = lax.optimization_barrier((small, input_grad))
    g_small, many, g1_in, g1_out = scatter_each(
        [
            (mixed, low2), (hid3, d_doubled),
            (hid2, d_q), (key_hid, d_k), (key_hid, d_v), (waves, d_r),
        ],
        d_before1, active1, hid1, low1, small,
    )

    sum_one = sum_one.astype(F32)
    w = width
    h = hidden_width
    gains = [g_small[:, TAPS + i] for i in range(8)]
    return (
        layer_out[None],
        input_grad[None],
        gains[0],
        g1_in,
        g1_out,
        gains[1],
        many[3],
        many[4],
        many[5],
        many[6],
        gains[2],
        gains[3],
        many[0],
        gains[4],
        jnp.concatenate([many[1], many[2]], axis=1),
        g_small[:, :TAPS].T,
        gains[5],
        sum_one[:, 2 * h :],
        gains[6],
        unpack_in(sum_one[:, :h], count),
        unpack_out(sum_one[:, h : 2 * h], w),
        gains[7],
    )


def solution(mesh):
    both = ("items", "seq")
    lead = P("items", "seq", None)
    group = P("items", None)
    flat = P(both)
    tall = P(both, None)
    side = P(None, both)
    return jax.shard_map(
        body,
        mesh=mesh,
        in_specs=(
            lead, group, group,
            flat, tall, tall, flat, tall, tall, tall, tall, flat, flat, tall,
            flat, tall, side, flat, tall, flat, tall, tall, flat,
            lead,
        ),
        out_specs=(
            lead, lead,
            flat, tall, tall, flat, tall, tall, tall, tall, flat, flat, tall,
            flat, tall, side, flat, tall, flat, tall, tall, flat,
        ),
        check_vma=False,
    )
```
